32 devices in a mesh: shot: 4 (over y, core), rcv: 8 (over z, x).
Axes of the slice: x: 2, y: 2, z: 4, core: 2. Of those that a mesh axis runs over, the one named last changes fastest.
Arguments:
- traces: bfloat16 [4, 8, 1536, 2048], P('shot', 'rcv'), may hold values from -6 to 6
- trace_shot: int32 [4, 8, 1536], P('shot', 'rcv'), may hold values from 0 to 127, as said below
- trace_rcv: int32 [4, 8, 1536], P('shot', 'rcv'), may hold values from 0 to 127
- fold_count: int32 [4, 8], P('shot', 'rcv'), may hold values from 512 to 1536
Outputs:
- shot_terms: float32 [512, 1024], P('shot')
- rcv_terms: float32 [1024, 1024], P('rcv')
The draws below stay inside these ranges and needn't reach their ends.
Inputs may be any that keep to these rules, and one draw needn't show every extreme that they name: `trace_shot`: in every tile, slot k < 128 holds a distinct shot, and its receiver index equals its shot index, so every shot and receiver of the tile's blocks has a live trace there.
All inputs are finite; a program needn't handle non-finite values.
Results may differ from the reference program's by a relative error of at most 0.0072.
Values sent between devices are 32-bit elements; how exact they have to be, the bound alone decides.
No kernel may reach another device: no remote copies, remote signals or barrier semaphores. Data moves between devices by JAX's collectives and lax.ppermute only.
A program may use at most 128 MiB of HBM per device.

```python
import jax
import jax.numpy as jnp
from jax import lax

SAMPLES = 2048
FREQS = 1024
SHOT_DEV = 128
RCV_DEV = 128
TRACE_DEV = 1536
SWEEPS = 3
N_SHOT = 4
N_RCV = 8


def slot_layout(key):
    base_key = jax.random.fold_in(key, 7)
    slots = jnp.arange(TRACE_DEV, dtype=jnp.int32)[None, None, :]
    shifts = jax.random.randint(jax.random.fold_in(base_key, 1), (N_SHOT, N_RCV, 1), 0, SHOT_DEV)
    random_shot = jax.random.randint(jax.random.fold_in(base_key, 2), (N_SHOT, N_RCV, TRACE_DEV), 0, SHOT_DEV)
    offsets = jax.random.randint(jax.random.fold_in(base_key, 3), (N_SHOT, N_RCV, TRACE_DEV), -4, 5)
    first_rows = slots < SHOT_DEV
    shot_index = jnp.where(first_rows, (slots + shifts) % SHOT_DEV, random_shot)
    offsets = jnp.where(first_rows, 0, offsets)
    rcv_index = (shot_index + offsets + RCV_DEV) % RCV_DEV
    return (shot_index.astype(jnp.int32), rcv_index.astype(jnp.int32))


def draw_trace_shot(key, part):
    return slot_layout(key)[0]


def draw_trace_rcv(key, part):
    return slot_layout(key)[1]


def draw_fold_count(key, part):
    count_key = jax.random.fold_in(key, 11)
    return jax.random.randint(count_key, (N_SHOT, N_RCV), TRACE_DEV // 3, TRACE_DEV + 1).astype(jnp.int32)


def levels(own_key, dims, split, low, top_value):
    gain = 1.0
    for axis_at, parts in split:
        draws = jax.random.uniform(jax.random.fold_in(jax.random.fold_in(own_key, 6), axis_at), (parts,), jnp.float32, low / len(split), top_value / len(split))
        gain = gain * jnp.repeat(jnp.exp(draws), dims[axis_at] // parts).reshape((-1,) + (1,) * (len(dims) - 1 - axis_at))
    return gain


def scatter_about(stream_key, extent, spread, most, shards=(), held_as=jnp.bfloat16):
    array = spread * jax.random.normal(stream_key, extent, jnp.float32)
    if shards:
        array = array * levels(stream_key, extent, shards, -0.22, 0.18)
    return jnp.clip(array, -most, most).astype(held_as)


def setup_inputs(seed: int = 0) -> dict:
    streams_of = jax.random.split(jax.random.key(seed), 5)
    traces = scatter_about(streams_of[0], (N_SHOT, N_RCV, TRACE_DEV, SAMPLES), 1.0, 6.0, ((0, 4), (1, 8)))
    trace_shot = draw_trace_shot(jax.random.fold_in(streams_of[4], 71), 0)
    trace_rcv = draw_trace_rcv(jax.random.fold_in(streams_of[4], 71), 0)
    fold_count = draw_fold_count(jax.random.fold_in(streams_of[4], 71), 0)
    return dict(traces=traces, trace_shot=trace_shot, trace_rcv=trace_rcv, fold_count=fold_count)


def dft_tables():
    index_n = jnp.arange(SAMPLES, dtype=jnp.int32)
    index_f = jnp.arange(FREQS, dtype=jnp.int32)
    product = (index_n[:, None] * index_f[None, :]) % SAMPLES
    angle_table = (2.0 * jnp.pi / SAMPLES) * product.astype(jnp.float32)
    return jnp.cos(angle_table).astype(jnp.bfloat16), jnp.sin(angle_table).astype(jnp.bfloat16)


def reference(traces, trace_shot, trace_rcv, fold_count):
    cos_table, sin_table = dft_tables()
    tiles_total = N_SHOT * N_RCV
    flat_traces = traces.reshape(tiles_total, TRACE_DEV, SAMPLES)
    flat_shot = trace_shot.reshape(tiles_total, TRACE_DEV)
    flat_rcv = trace_rcv.reshape(tiles_total, TRACE_DEV)
    flat_count = fold_count.reshape(tiles_total)

    def tile_sums(packed):
        tile_traces, tile_shot, tile_rcv, tile_count = packed
        real = jnp.dot(tile_traces, cos_table, preferred_element_type=jnp.float32)
        imag = jnp.dot(tile_traces, sin_table, preferred_element_type=jnp.float32)
        log_power = jnp.log((real * real + imag * imag) / SAMPLES + 1e-6)
        alive = (jnp.arange(TRACE_DEV, dtype=jnp.int32) < tile_count).astype(log_power.dtype)
        onehot_shot = (tile_shot[:, None] == jnp.arange(SHOT_DEV, dtype=jnp.int32)[None, :]).astype(log_power.dtype) * alive[:, None]
        onehot_rcv = (tile_rcv[:, None] == jnp.arange(RCV_DEV, dtype=jnp.int32)[None, :]).astype(log_power.dtype) * alive[:, None]
        shot_logs = jnp.dot(onehot_shot.T, log_power, precision=lax.Precision.HIGHEST)
        rcv_logs = jnp.dot(onehot_rcv.T, log_power, precision=lax.Precision.HIGHEST)
        pairs = jnp.dot(onehot_shot.T, onehot_rcv, precision=lax.Precision.HIGHEST)
        return shot_logs, rcv_logs, pairs

    shot_logs, rcv_logs, pairs = lax.map(tile_sums, (flat_traces, flat_shot, flat_rcv, flat_count))
    shot_logs = shot_logs.reshape(N_SHOT, N_RCV, SHOT_DEV, FREQS).sum(axis=1)
    rcv_logs = rcv_logs.reshape(N_SHOT, N_RCV, RCV_DEV, FREQS).sum(axis=0)
    pairs = pairs.reshape(N_SHOT, N_RCV, SHOT_DEV, RCV_DEV)
    shot_count = pairs.sum(axis=3).sum(axis=1)
    rcv_count = pairs.sum(axis=2).sum(axis=0)
    rcv_terms = jnp.zeros((N_RCV, RCV_DEV, FREQS), shot_logs.dtype)
    shot_terms = jnp.zeros((N_SHOT, SHOT_DEV, FREQS), shot_logs.dtype)
    for iteration in range(SWEEPS):
        shot_total = shot_logs - jnp.einsum("ijxy,jyf->ixf", pairs, rcv_terms, precision=lax.Precision.HIGHEST)
        shot_terms = shot_total / shot_count[:, :, None]
        rcv_total = rcv_logs - jnp.einsum("ijxy,ixf->jyf", pairs, shot_terms, precision=lax.Precision.HIGHEST)
        rcv_terms = rcv_total / rcv_count[:, :, None]
    return shot_terms.reshape(N_SHOT * SHOT_DEV, FREQS), rcv_terms.reshape(N_RCV * RCV_DEV, FREQS)
```

```python
import functools

import jax
import jax.numpy as jnp
import numpy as np
from jax import lax
from jax.experimental import pallas as pl
from jax.experimental.pallas import tpu as pltpu
from jax.sharding import PartitionSpec as P

SHOT_DEV = 128
RCV_DEV = 128
SWEEPS = 3
SLOT_BLOCK = 256
BIN_BLOCK = 256
ROW_BLOCK = 128
VMEM_BYTES = 48 * 1024 * 1024


def dft_tables(samples_count, bins_count):
    product = (np.arange(bins_count)[:, None] * np.arange(samples_count)[None, :]) % samples_count
    angle = (np.float32(2.0 * np.pi / samples_count) * product.astype(np.float32)).astype(np.float64)
    both = np.stack([np.cos(angle), np.sin(angle)]).astype(np.float32)
    return both.astype(jnp.bfloat16)


def across(a, b):
    return lax.dot_general(a, b, (((1,), (1,)), ((), ())), preferred_element_type=jnp.float32)


def along(a, b):
    return lax.dot_general(a, b, (((1,), (0,)), ((), ())), preferred_element_type=jnp.float32)


def spectra_kernel(inv_samples, traces_ref, table_ref, index_ref, shot_ref, rcv_ref):
    step = pl.program_id(1)
    block = traces_ref[...]
    slots = block.shape[0]
    rows = lax.broadcasted_iota(jnp.int32, (SHOT_DEV, slots), 0)
    onehot = jnp.concatenate(
        [(index_ref[k : k + 1, :] == rows).astype(jnp.float32) for k in range(2)], axis=0
    ).astype(jnp.bfloat16)

    @pl.when(step == 0)
    def _():
        shot_ref[...] = jnp.zeros_like(shot_ref)
        rcv_ref[...] = jnp.zeros_like(rcv_ref)

    for at in range(0, table_ref.shape[1], ROW_BLOCK):
        real = across(table_ref[0, at : at + ROW_BLOCK, :], block)
        imag = across(table_ref[1, at : at + ROW_BLOCK, :], block)
        logs = jnp.log((real * real + imag * imag) * inv_samples + 1e-06)
        high = logs.astype(jnp.bfloat16)
        low = (logs - high.astype(jnp.float32)).astype(jnp.bfloat16)
        sums = across(high, onehot) + across(low, onehot)
        shot_ref[at : at + ROW_BLOCK, :] += sums[:, :SHOT_DEV]
        rcv_ref[at : at + ROW_BLOCK, :] += sums[:, SHOT_DEV:]


def spectra_sums(traces, table, index):
    slots, samples = traces.shape
    bins = table.shape[1]
    return pl.pallas_call(
        functools.partial(spectra_kernel, 1.0 / samples),
        grid=(bins // BIN_BLOCK, slots // SLOT_BLOCK),
        in_specs=[
            pl.BlockSpec((SLOT_BLOCK, samples), lambda b, t: (t, 0)),
            pl.BlockSpec((2, BIN_BLOCK, samples), lambda b, t: (0, b, 0)),
            pl.BlockSpec((2, SLOT_BLOCK), lambda b, t: (0, t)),
        ],
        out_specs=[
            pl.BlockSpec((BIN_BLOCK, SHOT_DEV), lambda b, t: (b, 0)),
            pl.BlockSpec((BIN_BLOCK, RCV_DEV), lambda b, t: (b, 0)),
        ],
        out_shape=[
            jax.ShapeDtypeStruct((bins, SHOT_DEV), jnp.float32),
            jax.ShapeDtypeStruct((bins, RCV_DEV), jnp.float32),
        ],
        compiler_params=pltpu.CompilerParams(vmem_limit_bytes=VMEM_BYTES),
        cost_estimate=pl.CostEstimate(
            flops=4 * slots * samples * bins, bytes_accessed=32 * 1024 * 1024, transcendentals=slots * bins
        ),
    )(traces, table, index)


def pairs_kernel(shot_blocks, rcv_blocks, index_ref, high_ref, low_ref, shot_count_ref, rcv_count_ref):
    slots = index_ref.shape[2]
    rows = lax.broadcasted_iota(jnp.int32, (SHOT_DEV, slots), 0)

    for i in range(shot_blocks):

        def tile(j, carry):
            entry = index_ref[i * rcv_blocks + j]
            of_shot = (entry[0:1, :] == rows).astype(jnp.float32).astype(jnp.bfloat16)
            of_rcv = (entry[1:2, :] == rows).astype(jnp.float32).astype(jnp.bfloat16)
            pairs = across(of_shot, of_rcv)
            high = pairs.astype(jnp.bfloat16)
            low = (pairs - high.astype(jnp.float32)).astype(jnp.bfloat16)
            at = pl.ds(pl.multiple_of(j * RCV_DEV, RCV_DEV), RCV_DEV)
            high_ref[i * SHOT_DEV : (i + 1) * SHOT_DEV, at] = high
            low_ref[i * SHOT_DEV : (i + 1) * SHOT_DEV, at] = low
            return carry

        lax.fori_loop(0, rcv_blocks, tile, 0)
    ones_rcv = jnp.ones((16, rcv_blocks * RCV_DEV), jnp.bfloat16)
    ones_shot = jnp.ones((16, shot_blocks * SHOT_DEV), jnp.bfloat16)
    shot_count_ref[...] = (across(ones_rcv, high_ref[...]) + across(ones_rcv, low_ref[...]))[:8]
    rcv_count_ref[...] = (along(ones_shot, high_ref[...]) + along(ones_shot, low_ref[...]))[:8]


def pair_counts(index_every, shot_blocks, rcv_blocks):
    shots, rcvs = shot_blocks * SHOT_DEV, rcv_blocks * RCV_DEV
    return pl.pallas_call(
        functools.partial(pairs_kernel, shot_blocks, rcv_blocks),
        out_shape=[
            jax.ShapeDtypeStruct((shots, rcvs), jnp.bfloat16),
            jax.ShapeDtypeStruct((shots, rcvs), jnp.bfloat16),
            jax.ShapeDtypeStruct((8, shots), jnp.float32),
            jax.ShapeDtypeStruct((8, rcvs), jnp.float32),
        ],
        compiler_params=pltpu.CompilerParams(vmem_limit_bytes=VMEM_BYTES),
        cost_estimate=pl.CostEstimate(
            flops=2 * shots * rcvs * index_every.shape[2], bytes_accessed=4 * shots * rcvs, transcendentals=0
        ),
    )(index_every)


def solve_kernel(
    shot_blocks, rcv_blocks, shot_parts, rcv_parts, high_ref, low_ref, shot_count_ref, rcv_count_ref, shot_out, rcv_out
):
    bins = shot_parts.shape[1]

    def total(terms):
        return functools.reduce(lambda a, b: a + b, terms)

    shot_logs = jnp.concatenate(
        [total([shot_parts[i * rcv_blocks + j] for j in range(rcv_blocks)]) for i in range(shot_blocks)], axis=1
    )
    rcv_logs = jnp.concatenate(
        [total([rcv_parts[i * rcv_blocks + j] for i in range(shot_blocks)]) for j in range(rcv_blocks)], axis=1
    )
    shot_count = shot_count_ref[0:1, :]
    rcv_count = rcv_count_ref[0:1, :]

    def times(terms, product):
        first = terms.astype(jnp.bfloat16).astype(jnp.float32)
        rest = terms - first
        second = rest.astype(jnp.bfloat16).astype(jnp.float32)
        stack = jnp.concatenate([first, second, rest - second], axis=0).astype(jnp.bfloat16)
        out = product(stack, high_ref[...]) + product(stack, low_ref[...])
        return out[:bins] + out[bins : 2 * bins] + out[2 * bins :]

    shot_terms = shot_logs / shot_count
    rcv_terms = (rcv_logs - times(shot_terms, along)) / rcv_count
    for _ in range(SWEEPS - 1):
        shot_terms = (shot_logs - times(rcv_terms, across)) / shot_count
        rcv_terms = (rcv_logs - times(shot_terms, along)) / rcv_count
    for i in range(shot_blocks):
        shot_out[i] = shot_terms[:, i * SHOT_DEV : (i + 1) * SHOT_DEV]
    for j in range(rcv_blocks):
        rcv_out[j] = rcv_terms[:, j * RCV_DEV : (j + 1) * RCV_DEV]


def solve(shot_parts, rcv_parts, counts, shot_blocks, rcv_blocks):
    bins = shot_parts.shape[1]
    return pl.pallas_call(
        functools.partial(solve_kernel, shot_blocks, rcv_blocks),
        out_shape=[
            jax.ShapeDtypeStruct((shot_blocks, bins, SHOT_DEV), jnp.float32),
            jax.ShapeDtypeStruct((rcv_blocks, bins, RCV_DEV), jnp.float32),
        ],
        compiler_params=pltpu.CompilerParams(vmem_limit_bytes=VMEM_BYTES),
    )(shot_parts, rcv_parts, *counts)


def shards(traces, trace_shot, trace_rcv, fold_count):
    slot_total = traces.shape[2]
    samples_count = traces.shape[3]
    bins_count = samples_count // 2
    shot_blocks = lax.axis_size("shot")
    rcv_blocks = lax.axis_size("rcv")
    device_total = shot_blocks * rcv_blocks
    owned_bins = bins_count // device_total
    axes = ("shot", "rcv")
    table = jnp.asarray(dft_tables(samples_count, bins_count))
    alive = jnp.arange(slot_total, dtype=jnp.int32) < fold_count[0, 0]
    index = jnp.where(alive, jnp.stack([trace_shot[0, 0], trace_rcv[0, 0]]), -1)
    index_every = lax.all_to_all(
        jnp.broadcast_to(index[None], (device_total,) + index.shape), axes, split_axis=0, concat_axis=0, tiled=True
    )
    shot_logs, rcv_logs = spectra_sums(traces[0, 0], table, index)
    counts = pair_counts(index_every, shot_blocks, rcv_blocks)
    exchange = functools.partial(lax.all_to_all, axis_name=axes, split_axis=0, concat_axis=0, tiled=True)
    shot_parts = exchange(shot_logs.reshape(device_total, owned_bins, SHOT_DEV))
    rcv_parts = exchange(rcv_logs.reshape(device_total, owned_bins, RCV_DEV))
    shot_local, rcv_local = solve(shot_parts, rcv_parts, counts, shot_blocks, rcv_blocks)
    shot_send = jnp.broadcast_to(shot_local[:, None], (shot_blocks, rcv_blocks, owned_bins, SHOT_DEV))
    rcv_send = jnp.broadcast_to(rcv_local[None], (shot_blocks, rcv_blocks, owned_bins, RCV_DEV))
    shot_back = exchange(shot_send.reshape(device_total, owned_bins, SHOT_DEV))
    rcv_back = exchange(rcv_send.reshape(device_total, owned_bins, RCV_DEV))
    return shot_back.reshape(bins_count, SHOT_DEV).T, rcv_back.reshape(bins_count, RCV_DEV).T


def solution(mesh):
    return jax.shard_map(
        shards,
        mesh=mesh,
        in_specs=(
            P("shot", "rcv", None, None),
            P("shot", "rcv", None),
            P("shot", "rcv", None),
            P("shot", "rcv"),
        ),
        out_specs=(P("shot", None), P("rcv", None)),
        check_vma=False,
    )
```

```python
import functools

import jax
import jax.numpy as jnp
import numpy as np
from jax import lax
from jax.experimental import pallas as pl
from jax.experimental.pallas import tpu as pltpu
from jax.sharding import PartitionSpec as P

SHOT_DEV = 128
RCV_DEV = 128
SWEEPS = 3
GROUPS = 2
ROW_BLOCK = 256
SLOT_BLOCK = 512
VMEM_BYTES = 40 * 1024 * 1024
WHOLE_VMEM_BYTES = 62 * 1024 * 1024


def dft_tables(samples_count, bins_count):
    product = (np.arange(bins_count)[:, None] * np.arange(samples_count)[None, :]) % samples_count
    angle = (np.float32(2.0 * np.pi / samples_count) * product.astype(np.float32)).astype(np.float64)
    both = np.stack([np.cos(angle), np.sin(angle)]).astype(np.float32)
    return both.astype(jnp.bfloat16)


def across(a, b):
    return lax.dot_general(a, b, (((1,), (1,)), ((), ())), preferred_element_type=jnp.float32)


def along(a, b):
    return lax.dot_general(a, b, (((1,), (0,)), ((), ())), preferred_element_type=jnp.float32)


def spectra_kernel(inv_samples, traces_hbm, table_hbm, index_ref, sums_ref, traces_ref, table_ref, trace_sem, table_sem):
    slots = traces_ref.shape[0]
    bins = table_ref.shape[1]

    def trace_copy(at):
        span = pl.ds(at, SLOT_BLOCK)
        return pltpu.make_async_copy(traces_hbm.at[span], traces_ref.at[span], trace_sem.at[at // SLOT_BLOCK])

    def table_copy(at):
        span = pl.ds(at, ROW_BLOCK)
        return pltpu.make_async_copy(table_hbm.at[:, span], table_ref.at[:, span], table_sem.at[at // ROW_BLOCK])

    table_copy(0).start()
    for at in range(0, slots, SLOT_BLOCK):
        trace_copy(at).start()
    for at in range(ROW_BLOCK, bins, ROW_BLOCK):
        table_copy(at).start()
    rows = lax.broadcasted_iota(jnp.int32, (SHOT_DEV, slots), 0)
    onehot = jnp.concatenate(
        [(index_ref[k : k + 1, :] == rows).astype(jnp.float32) for k in range(2)], axis=0
    ).astype(jnp.bfloat16)

    def block_sums(at, first, last):
        block = traces_ref[first:last, :]
        real = across(table_ref[0, at : at + ROW_BLOCK, :], block)
        imag = across(table_ref[1, at : at + ROW_BLOCK, :], block)
        logs = jnp.log((real * real + imag * imag) * inv_samples + 1e-06)
        high = logs.astype(jnp.bfloat16)
        low = (logs - high.astype(jnp.float32)).astype(jnp.bfloat16)
        return across(high, onehot[:, first:last]) + across(low, onehot[:, first:last])

    table_copy(0).wait()
    for first in range(0, slots, SLOT_BLOCK):
        trace_copy(first).wait()
        sums = block_sums(0, first, first + SLOT_BLOCK)
        if first == 0:
            sums_ref[:ROW_BLOCK, :] = sums
        else:
            sums_ref[:ROW_BLOCK, :] += sums
    for at in range(ROW_BLOCK, bins, ROW_BLOCK):
        table_copy(at).wait()
        sums_ref[at : at + ROW_BLOCK, :] = block_sums(at, 0, slots)


def spectra_sums(traces, table, index):
    slots, samples = traces.shape
    bins = table.shape[1]
    return pl.pallas_call(
        functools.partial(spectra_kernel, 1.0 / samples),
        in_specs=[
            pl.BlockSpec(memory_space=pltpu.HBM),
            pl.BlockSpec(memory_space=pltpu.HBM),
            pl.BlockSpec(memory_space=pltpu.VMEM),
        ],
        out_specs=pl.BlockSpec(memory_space=pltpu.VMEM),
        out_shape=jax.ShapeDtypeStruct((bins, SHOT_DEV + RCV_DEV), jnp.float32),
        scratch_shapes=[
            pltpu.VMEM(traces.shape, traces.dtype),
            pltpu.VMEM(table.shape, table.dtype),
            pltpu.SemaphoreType.DMA((slots // SLOT_BLOCK,)),
            pltpu.SemaphoreType.DMA((bins // ROW_BLOCK,)),
        ],
        compiler_params=pltpu.CompilerParams(vmem_limit_bytes=WHOLE_VMEM_BYTES),
        cost_estimate=pl.CostEstimate(
            flops=4 * slots * samples * bins, bytes_accessed=4 * samples * bins, transcendentals=slots * bins
        ),
    )(traces, table, index)


def pairs_kernel(shot_blocks, rcv_blocks, index_ref, high_ref, low_ref, shot_count_ref, rcv_count_ref):
    slots = index_ref.shape[2]
    rows = lax.broadcasted_iota(jnp.int32, (SHOT_DEV, slots), 0)

    for i in range(shot_blocks):

        def tile(j, carry):
            entry = index_ref[i * rcv_blocks + j]
            of_shot = (entry[0:1, :] == rows).astype(jnp.float32).astype(jnp.bfloat16)
            of_rcv = (entry[1:2, :] == rows).astype(jnp.float32).astype(jnp.bfloat16)
            pairs = across(of_shot, of_rcv)
            high = pairs.astype(jnp.bfloat16)
            low = (pairs - high.astype(jnp.float32)).astype(jnp.bfloat16)
            at = pl.ds(pl.multiple_of(j * RCV_DEV, RCV_DEV), RCV_DEV)
            high_ref[i * SHOT_DEV : (i + 1) * SHOT_DEV, at] = high
            low_ref[i * SHOT_DEV : (i + 1) * SHOT_DEV, at] = low
            return carry

        lax.fori_loop(0, rcv_blocks, tile, 0)
    ones_rcv = jnp.ones((16, rcv_blocks * RCV_DEV), jnp.bfloat16)
    ones_shot = jnp.ones((16, shot_blocks * SHOT_DEV), jnp.bfloat16)
    shot_count_ref[...] = (across(ones_rcv, high_ref[...]) + across(ones_rcv, low_ref[...]))[:8]
    rcv_count_ref[...] = (along(ones_shot, high_ref[...]) + along(ones_shot, low_ref[...]))[:8]


def pair_counts(index_every, shot_blocks, rcv_blocks):
    shots, rcvs = shot_blocks * SHOT_DEV, rcv_blocks * RCV_DEV
    return pl.pallas_call(
        functools.partial(pairs_kernel, shot_blocks, rcv_blocks),
        out_shape=[
            jax.ShapeDtypeStruct((shots, rcvs), jnp.bfloat16),
            jax.ShapeDtypeStruct((shots, rcvs), jnp.bfloat16),
            jax.ShapeDtypeStruct((8, shots), jnp.float32),
            jax.ShapeDtypeStruct((8, rcvs), jnp.float32),
        ],
        compiler_params=pltpu.CompilerParams(vmem_limit_bytes=VMEM_BYTES),
        cost_estimate=pl.CostEstimate(
            flops=2 * shots * rcvs * index_every.shape[2], bytes_accessed=4 * shots * rcvs, transcendentals=0
        ),
    )(index_every)


def solve_kernel(shot_blocks, rcv_blocks, groups, *refs):
    high_ref, low_ref, shot_count_ref, rcv_count_ref, out = refs[groups:]
    bins = out.shape[1]

    def total(places, lanes):
        sums = [functools.reduce(lambda a, b: a + b, [part[k, :, lanes] for k in places]) for part in refs[:groups]]
        return jnp.concatenate(sums, axis=0)

    of_shot, of_rcv = slice(0, SHOT_DEV), slice(SHOT_DEV, SHOT_DEV + RCV_DEV)
    shot_logs = jnp.concatenate(
        [total([i * rcv_blocks + j for j in range(rcv_blocks)], of_shot) for i in range(shot_blocks)], axis=1
    )
    rcv_logs = jnp.concatenate(
        [total([i * rcv_blocks + j for i in range(shot_blocks)], of_rcv) for j in range(rcv_blocks)], axis=1
    )
    shot_count = shot_count_ref[0:1, :]
    rcv_count = rcv_count_ref[0:1, :]

    def times(terms, product):
        first = terms.astype(jnp.bfloat16).astype(jnp.float32)
        rest = terms - first
        second = rest.astype(jnp.bfloat16).astype(jnp.float32)
        stack = jnp.concatenate([first, second, rest - second], axis=0).astype(jnp.bfloat16)
        out = product(stack, high_ref[...]) + product(stack, low_ref[...])
        return out[:bins] + out[bins : 2 * bins] + out[2 * bins :]

    shot_terms = shot_logs / shot_count
    rcv_terms = (rcv_logs - times(shot_terms, along)) / rcv_count
    for _ in range(SWEEPS - 1):
        shot_terms = (shot_logs - times(rcv_terms, across)) / shot_count
        rcv_terms = (rcv_logs - times(shot_terms, along)) / rcv_count
    for i in range(shot_blocks):
        for j in range(rcv_blocks):
            out[i * rcv_blocks + j, :, :SHOT_DEV] = shot_terms[:, i * SHOT_DEV : (i + 1) * SHOT_DEV]
            out[i * rcv_blocks + j, :, SHOT_DEV:] = rcv_terms[:, j * RCV_DEV : (j + 1) * RCV_DEV]


def solve(parts, counts, shot_blocks, rcv_blocks):
    devices, bins, lanes = parts[0].shape
    whole = (devices, bins * len(parts), lanes)
    return pl.pallas_call(
        functools.partial(solve_kernel, shot_blocks, rcv_blocks, len(parts)),
        out_shape=jax.ShapeDtypeStruct(whole, jnp.float32),
        compiler_params=pltpu.CompilerParams(vmem_limit_bytes=VMEM_BYTES),
    )(*parts, *counts)


def turn_kernel(groups, back, shot_out, rcv_out):
    devices, owned, lanes = back.shape
    part = owned // groups
    for g in range(groups):
        block = back[:, g * part : (g + 1) * part, :].reshape(devices * part, lanes)
        at = slice(g * devices * part, (g + 1) * devices * part)
        shot_out[:, at] = block[:, :SHOT_DEV].T
        rcv_out[:, at] = block[:, SHOT_DEV:].T


def turn(back, groups):
    bins = back.shape[0] * back.shape[1]
    return pl.pallas_call(
        functools.partial(turn_kernel, groups),
        out_shape=[
            jax.ShapeDtypeStruct((SHOT_DEV, bins), jnp.float32),
            jax.ShapeDtypeStruct((RCV_DEV, bins), jnp.float32),
        ],
        compiler_params=pltpu.CompilerParams(vmem_limit_bytes=VMEM_BYTES),
    )(back)


def shards(traces, trace_shot, trace_rcv, fold_count):
    slot_total = traces.shape[2]
    samples_count = traces.shape[3]
    bins_count = samples_count // 2
    shot_blocks = lax.axis_size("shot")
    rcv_blocks = lax.axis_size("rcv")
    device_total = shot_blocks * rcv_blocks
    groups = GROUPS
    while bins_count % (groups * device_total * 8):
        groups //= 2
    group_bins = bins_count // groups
    exchange = functools.partial(
        lax.all_to_all, axis_name=("shot", "rcv"), split_axis=0, concat_axis=0, tiled=True
    )
    table = dft_tables(samples_count, bins_count)
    alive = jnp.arange(slot_total, dtype=jnp.int32) < fold_count[0, 0]
    index = jnp.where(alive, jnp.stack([trace_shot[0, 0], trace_rcv[0, 0]]), -1)
    index_every = exchange(jnp.broadcast_to(index[None], (device_total,) + index.shape))
    parts = []
    for g in range(groups):
        sums = spectra_sums(traces[0, 0], jnp.asarray(table[:, g * group_bins : (g + 1) * group_bins]), index)
        parts.append(exchange(sums.reshape(device_total, group_bins // device_total, SHOT_DEV + RCV_DEV)))
    counts = pair_counts(index_every, shot_blocks, rcv_blocks)
    back = exchange(solve(parts, counts, shot_blocks, rcv_blocks))
    return tuple(turn(back, groups))


def solution(mesh):
    return jax.shard_map(
        shards,
        mesh=mesh,
        in_specs=(
            P("shot", "rcv", None, None),
            P("shot", "rcv", None),
            P("shot", "rcv", None),
            P("shot", "rcv"),
        ),
        out_specs=(P("shot", None), P("rcv", None)),
        check_vma=False,
    )
```

```python
import functools

import jax
import jax.numpy as jnp
import numpy as np
from jax import lax
from jax.experimental import pallas as pl
from jax.experimental.pallas import tpu as pltpu
from jax.sharding import PartitionSpec as P

SHOT_DEV = 128
RCV_DEV = 128
SWEEPS = 3
OWN_ROWS = 8
LANES = 256
ROW_BLOCK = 256
SLOT_BLOCK = 512
VMEM_BYTES = 40 * 1024 * 1024
WHOLE_VMEM_BYTES = 62 * 1024 * 1024


def dft_tables(samples_count, bins_count):
    product = (np.arange(bins_count)[:, None] * np.arange(samples_count)[None, :]) % samples_count
    angle = (np.float32(2.0 * np.pi / samples_count) * product.astype(np.float32)).astype(np.float64)
    both = np.stack([np.cos(angle), np.sin(angle)]).astype(np.float32)
    both = both.reshape(2, bins_count // ROW_BLOCK, ROW_BLOCK, samples_count).transpose(1, 0, 2, 3)
    return both.reshape(-1, 2 * ROW_BLOCK, samples_count).astype(jnp.bfloat16)


def across(a, b):
    return lax.dot_general(a, b, (((1,), (1,)), ((), ())), preferred_element_type=jnp.float32)


def along(a, b):
    return lax.dot_general(a, b, (((1,), (0,)), ((), ())), preferred_element_type=jnp.float32)


def index_lines(slots):
    lines = slots // (2 * LANES)
    return lines, -(-2 * lines // OWN_ROWS) * OWN_ROWS


def spectra_kernel(
    shot_blocks, inv_samples, traces_hbm, table_hbm, shot_ref, rcv_ref, count_ref, sums_ref, traces_ref, table_ref, trace_sem, table_sem
):
    slots = traces_ref.shape[0]
    blocks = table_ref.shape[0]
    pieces = slots // SLOT_BLOCK

    def trace_copy(k):
        span = pl.ds(k * SLOT_BLOCK, SLOT_BLOCK)
        return pltpu.make_async_copy(traces_hbm.at[span], traces_ref.at[span], trace_sem.at[k])

    def table_copy(k):
        return pltpu.make_async_copy(table_hbm.at[k], table_ref.at[k], table_sem.at[k])

    copies = [table_copy(0)] + [trace_copy(k) for k in range(pieces)] + [table_copy(k) for k in range(1, blocks)]
    arrived = []

    def bring(count):
        while len(arrived) < count:
            k = len(arrived)
            if k + 2 < len(copies):
                copies[k + 2].start()
            copies[k].wait()
            arrived.append(k)

    copies[0].start()
    copies[1].start()
    rows = lax.broadcasted_iota(jnp.int32, (SHOT_DEV, slots), 0)
    alive = lax.broadcasted_iota(jnp.int32, (1, slots), 1) < count_ref[0, 0]
    indices = [jnp.where(alive, ref[...], -1) for ref in (shot_ref, rcv_ref)]
    onehot = jnp.concatenate([(index == rows).astype(jnp.float32) for index in indices], axis=0).astype(jnp.bfloat16)
    if shot_blocks:
        lines, taken = index_lines(slots)
        for i in range(shot_blocks):
            ends = [(i % 2 * lines + k) * LANES for k in range(lines)]
            text = [index[:, at : at + LANES].astype(jnp.float32) for index in indices for at in ends]
            text.append(jnp.zeros((taken - 2 * lines, LANES), jnp.float32))
            wide = sums_ref.shape[0] // shot_blocks
            sums_ref[i * wide : (i + 1) * wide, OWN_ROWS:, :] = jnp.broadcast_to(
                jnp.concatenate(text, axis=0)[None], (wide, taken, LANES)
            )

    def add_up(unit, both):
        row, start, stop = unit
        real, imag = both[:ROW_BLOCK], both[ROW_BLOCK:]
        logs = jnp.log((real * real + imag * imag) * inv_samples + 1e-06)
        high = logs.astype(jnp.bfloat16)
        low = (logs - high.astype(jnp.float32)).astype(jnp.bfloat16)
        sums = across(high, onehot[:, start:stop]) + across(low, onehot[:, start:stop])
        if shot_blocks:
            owners = ROW_BLOCK // OWN_ROWS
            at = (slice(row * owners, (row + 1) * owners), slice(0, OWN_ROWS), slice(None))
            sums = sums.reshape(owners, OWN_ROWS, LANES)
        else:
            at = (slice(row * ROW_BLOCK, (row + 1) * ROW_BLOCK), slice(None))
        if start == 0:
            sums_ref[at] = sums
        else:
            sums_ref[at] += sums

    units = [(0, k * SLOT_BLOCK, (k + 1) * SLOT_BLOCK) for k in range(pieces)]
    units += [(row, 0, slots) for row in range(1, blocks)]
    before = None
    for k, unit in enumerate(units):
        bring(2 + k)
        row, start, stop = unit
        both = across(table_ref[row], traces_ref[start:stop, :])
        if before is not None:
            add_up(*before)
        before = (unit, both)
    add_up(*before)


def spectra_sums(traces, table, trace_shot, trace_rcv, fold_count, shot_blocks=0):
    slots, samples = traces.shape
    blocks = table.shape[0]
    bins = blocks * ROW_BLOCK
    shape = (bins // OWN_ROWS, OWN_ROWS + index_lines(slots)[1], LANES) if shot_blocks else (bins, LANES)
    in_vmem = pl.BlockSpec(memory_space=pltpu.VMEM)
    in_hbm = pl.BlockSpec(memory_space=pltpu.HBM)
    return pl.pallas_call(
        functools.partial(spectra_kernel, shot_blocks, 1.0 / samples),
        in_specs=[in_hbm, in_hbm, in_vmem, in_vmem, pl.BlockSpec(memory_space=pltpu.SMEM)],
        out_specs=in_vmem,
        out_shape=jax.ShapeDtypeStruct(shape, jnp.float32),
        scratch_shapes=[
            pltpu.VMEM(traces.shape, traces.dtype),
            pltpu.VMEM(table.shape, table.dtype),
            pltpu.SemaphoreType.DMA((slots // SLOT_BLOCK,)),
            pltpu.SemaphoreType.DMA((blocks,)),
        ],
        compiler_params=pltpu.CompilerParams(vmem_limit_bytes=WHOLE_VMEM_BYTES),
        cost_estimate=pl.CostEstimate(
            flops=4 * slots * samples * bins, bytes_accessed=4 * samples * bins, transcendentals=slots * bins
        ),
    )(traces, table, trace_shot, trace_rcv, fold_count)


def pairs_kernel(lines, mine_ref, other_ref, high_ref, low_ref, shot_count_ref, rcv_count_ref):
    rcv_blocks = high_ref.shape[1] // RCV_DEV
    slots = 2 * lines * LANES
    rows = lax.broadcasted_iota(jnp.int32, (SHOT_DEV, slots), 0).astype(jnp.float32).astype(jnp.bfloat16)
    one = jnp.ones((SHOT_DEV, slots), jnp.bfloat16)
    zero = jnp.zeros_like(one)
    for tile in range(mine_ref.shape[0]):
        halves = [ref[tile] for ref in (mine_ref, other_ref)]
        onehots = []
        for first in (0, lines):
            flat = [half[first + k : first + k + 1, :] for half in halves for k in range(lines)]
            onehots.append(jnp.where(jnp.concatenate(flat, axis=1).astype(jnp.bfloat16) == rows, one, zero))
        pairs = across(*onehots)
        high = pairs.astype(jnp.bfloat16)
        i, j = divmod(tile, rcv_blocks)
        place = (slice(i * SHOT_DEV, (i + 1) * SHOT_DEV), slice(j * RCV_DEV, (j + 1) * RCV_DEV))
        high_ref[place] = high
        low_ref[place] = (pairs - high.astype(jnp.float32)).astype(jnp.bfloat16)
    ones_rcv = jnp.ones((16, high_ref.shape[1]), jnp.bfloat16)
    ones_shot = jnp.ones((16, high_ref.shape[0]), jnp.bfloat16)
    shot_count_ref[...] = (across(ones_rcv, high_ref[...]) + across(ones_rcv, low_ref[...]))[:8]
    rcv_count_ref[...] = (along(ones_shot, high_ref[...]) + along(ones_shot, low_ref[...]))[:8]


def pair_counts(mine, other, lines, shot_blocks, rcv_blocks):
    shots, rcvs = shot_blocks * SHOT_DEV, rcv_blocks * RCV_DEV
    return pl.pallas_call(
        functools.partial(pairs_kernel, lines),
        out_shape=[
            jax.ShapeDtypeStruct((shots, rcvs), jnp.bfloat16),
            jax.ShapeDtypeStruct((shots, rcvs), jnp.bfloat16),
            jax.ShapeDtypeStruct((8, shots), jnp.float32),
            jax.ShapeDtypeStruct((8, rcvs), jnp.float32),
        ],
        compiler_params=pltpu.CompilerParams(vmem_limit_bytes=VMEM_BYTES),
        cost_estimate=pl.CostEstimate(
            flops=4 * shots * rcvs * lines * LANES, bytes_accessed=4 * shots * rcvs, transcendentals=0
        ),
    )(mine, other)


def solve_kernel(shot_blocks, rcv_blocks, own_rows, *refs):
    groups = len(own_rows)
    high_ref, low_ref, shot_count_ref, rcv_count_ref, out = refs[groups:]
    bins = out.shape[1] * 2 // 3

    def total(places, lanes):
        sums = [
            functools.reduce(lambda a, b: a + b, [part[k, :count, lanes] for k in places])
            for part, count in zip(refs, own_rows)
        ]
        return jnp.concatenate(sums, axis=0)

    of_shot, of_rcv = slice(0, SHOT_DEV), slice(SHOT_DEV, SHOT_DEV + RCV_DEV)
    shot_logs = jnp.concatenate(
        [total([i * rcv_blocks + j for j in range(rcv_blocks)], of_shot) for i in range(shot_blocks)], axis=1
    )
    rcv_logs = jnp.concatenate(
        [total([i * rcv_blocks + j for i in range(shot_blocks)], of_rcv) for j in range(rcv_blocks)], axis=1
    )
    shot_count = shot_count_ref[0:1, :]
    rcv_count = rcv_count_ref[0:1, :]

    def times(terms, product):
        first = terms.astype(jnp.bfloat16).astype(jnp.float32)
        rest = terms - first
        second = rest.astype(jnp.bfloat16).astype(jnp.float32)
        stack = jnp.concatenate([first, second, rest - second], axis=0).astype(jnp.bfloat16)
        out = product(stack, high_ref[...]) + product(stack, low_ref[...])
        return out[:bins] + out[bins : 2 * bins] + out[2 * bins :]

    shot_terms = shot_logs / shot_count
    rcv_terms = (rcv_logs - times(shot_terms, along)) / rcv_count
    for _ in range(SWEEPS - 1):
        shot_terms = (shot_logs - times(rcv_terms, across)) / shot_count
        rcv_terms = (rcv_logs - times(shot_terms, along)) / rcv_count
    half = bins // 2
    for i in range(shot_blocks):
        mine = rcv_terms[(i % 2) * half : (i % 2 + 1) * half]
        for j in range(rcv_blocks):
            out[i * rcv_blocks + j, :bins, :] = shot_terms[:, i * SHOT_DEV : (i + 1) * SHOT_DEV]
            out[i * rcv_blocks + j, bins:, :] = mine[:, j * RCV_DEV : (j + 1) * RCV_DEV]


def solve(parts, counts, own_rows, shot_blocks, rcv_blocks):
    return pl.pallas_call(
        functools.partial(solve_kernel, shot_blocks, rcv_blocks, own_rows),
        out_shape=jax.ShapeDtypeStruct((parts[0].shape[0], sum(own_rows) * 3 // 2, SHOT_DEV), jnp.float32),
        compiler_params=pltpu.CompilerParams(vmem_limit_bytes=VMEM_BYTES),
    )(*parts, *counts)


def turn_kernel(own_rows, even_ref, back, other, shot_out, rcv_out):
    devices, owned = back.shape[0], back.shape[1] * 2 // 3
    mine = back[:, owned:, :]
    even = even_ref[0] == 1
    rcv_back = jnp.concatenate([jnp.where(even, mine, other[...]), jnp.where(even, other[...], mine)], axis=1)
    row, at = 0, 0
    for count in own_rows:
        rows, row = slice(row, row + count), row + count
        columns, at = slice(at, at + devices * count), at + devices * count
        shot_out[:, columns] = back[:, rows, :].reshape(devices * count, SHOT_DEV).T
        rcv_out[:, columns] = rcv_back[:, rows, :].reshape(devices * count, RCV_DEV).T


def turn(even, back, other, own_rows):
    bins = back.shape[0] * back.shape[1] * 2 // 3
    return pl.pallas_call(
        functools.partial(turn_kernel, own_rows),
        in_specs=[pl.BlockSpec(memory_space=pltpu.SMEM)] + [pl.BlockSpec(memory_space=pltpu.VMEM)] * 2,
        out_shape=[
            jax.ShapeDtypeStruct((SHOT_DEV, bins), jnp.float32),
            jax.ShapeDtypeStruct((RCV_DEV, bins), jnp.float32),
        ],
        compiler_params=pltpu.CompilerParams(vmem_limit_bytes=VMEM_BYTES),
    )(even, back, other)


def shards(traces, trace_shot, trace_rcv, fold_count):
    slot_total = traces.shape[2]
    samples_count = traces.shape[3]
    bins_count = samples_count // 2
    shot_blocks = lax.axis_size("shot")
    rcv_blocks = lax.axis_size("rcv")
    device_total = shot_blocks * rcv_blocks
    owned = bins_count // device_total
    own_rows = [OWN_ROWS] + ([owned - OWN_ROWS] if owned > OWN_ROWS else [])
    exchange = functools.partial(
        lax.all_to_all, axis_name=("shot", "rcv"), split_axis=0, concat_axis=0, tiled=True
    )
    swap = [(i, i ^ 1) for i in range(shot_blocks)]
    table = dft_tables(samples_count, bins_count)
    lines, taken = index_lines(slot_total)
    parts, at = [], 0
    for rows in own_rows:
        blocks = rows * device_total // ROW_BLOCK
        sums = spectra_sums(
            traces[0, 0],
            jnp.asarray(table[at : at + blocks]),
            trace_shot[0],
            trace_rcv[0],
            fold_count,
            0 if at else shot_blocks,
        )
        parts.append(exchange(sums if at == 0 else sums.reshape(device_total, rows, LANES)))
        at += blocks
    mine = parts[0][:, OWN_ROWS:, :]
    counts = pair_counts(mine, lax.ppermute(mine, "shot", swap), lines, shot_blocks, rcv_blocks)
    back = exchange(solve(parts, counts, own_rows, shot_blocks, rcv_blocks))
    other = lax.ppermute(back[:, owned:, :], "shot", swap)
    even = (1 - lax.axis_index("shot") % 2).astype(jnp.int32).reshape(1)
    return tuple(turn(even, back, other, own_rows))


def solution(mesh):
    return jax.shard_map(
        shards,
        mesh=mesh,
        in_specs=(
            P("shot", "rcv", None, None),
            P("shot", "rcv", None),
            P("shot", "rcv", None),
            P("shot", "rcv"),
        ),
        out_specs=(P("shot", None), P("rcv", None)),
        check_vma=False,
    )
```

```python
import functools

import jax
import jax.numpy as jnp
import numpy as np
from jax import lax
from jax.experimental import pallas as pl
from jax.experimental.pallas import tpu as pltpu
from jax.sharding import PartitionSpec as P

SHOT_DEV = 128
RCV_DEV = 128
SWEEPS = 3
OWN_ROWS = 8
LANES = 256
ROW_BLOCK = 256
SLOT_BLOCK = 512
VMEM_BYTES = 40 * 1024 * 1024
WHOLE_VMEM_BYTES = 62 * 1024 * 1024


FOLDS = 4
QUARTERS = (0, 2, 1, 3)


def dft_tables(samples_count, bins_count):
    bins = np.concatenate([np.arange(over, bins_count, FOLDS) for over in QUARTERS])
    product = (bins[:, None] * np.arange(samples_count)[None, :]) % samples_count
    angle = (np.float32(2.0 * np.pi / samples_count) * product.astype(np.float32)).astype(np.float64)
    both = np.stack([np.cos(angle), np.sin(angle)]).astype(np.float32)
    both = both.reshape(2, bins_count // ROW_BLOCK, ROW_BLOCK, samples_count).transpose(1, 0, 2, 3)
    both = both.reshape(-1, 2 * ROW_BLOCK, samples_count).astype(jnp.bfloat16)
    even = bins_count // ROW_BLOCK // 2
    return both[:even, :, : samples_count // FOLDS], both[even:]


def across(a, b):
    return lax.dot_general(a, b, (((1,), (1,)), ((), ())), preferred_element_type=jnp.float32)


def along(a, b):
    return lax.dot_general(a, b, (((1,), (0,)), ((), ())), preferred_element_type=jnp.float32)


def index_lines(slots):
    lines = slots // (2 * LANES)
    return lines, -(-2 * lines // OWN_ROWS) * OWN_ROWS


def spectra_kernel(shot_blocks, inv_samples, folds, counts, traces_hbm, *refs):
    tables = len(counts)
    table_hbms, refs = refs[:tables], refs[tables:]
    shot_ref, rcv_ref, count_ref, sums_ref, traces_ref, folded_ref, trace_sem = refs[:7]
    table_refs, table_sems = refs[7 : 7 + tables], refs[7 + tables :]
    slots, samples = traces_ref.shape
    pieces = slots // SLOT_BLOCK
    spans = [(k * SLOT_BLOCK, (k + 1) * SLOT_BLOCK) for k in range(pieces)]

    def trace_copy(k):
        span = pl.ds(k * SLOT_BLOCK, SLOT_BLOCK)
        return pltpu.make_async_copy(traces_hbm.at[span], traces_ref.at[span], trace_sem.at[k])

    def table_copy(table, k):
        return pltpu.make_async_copy(table_hbms[table].at[k], table_refs[table].at[k], table_sems[table].at[k])

    blocks = [(table, k) for table in range(tables) for k in range(counts[table])]
    early = min(2, len(blocks))
    order = [blocks[0], 0] + blocks[1:early] + list(range(1, pieces)) + blocks[early:]
    copies = [table_copy(*what) if isinstance(what, tuple) else trace_copy(what) for what in order]
    arrived = []

    def bring(*needed):
        while len(arrived) <= max(order.index(what) for what in needed):
            k = len(arrived)
            if k + 2 < len(copies):
                copies[k + 2].start()
            copies[k].wait()
            arrived.append(k)

    copies[0].start()
    copies[1].start()
    rows = lax.broadcasted_iota(jnp.int32, (SHOT_DEV, slots), 0)
    alive = lax.broadcasted_iota(jnp.int32, (1, slots), 1) < count_ref[0, 0]
    indices = [jnp.where(alive, ref[...], -1) for ref in (shot_ref, rcv_ref)]
    onehot = jnp.concatenate([(index == rows).astype(jnp.float32) for index in indices], axis=0).astype(jnp.bfloat16)
    if shot_blocks:
        lines, taken = index_lines(slots)
        for i in range(shot_blocks):
            ends = [(i % 2 * lines + k) * LANES for k in range(lines)]
            text = [index[:, at : at + LANES].astype(jnp.float32) for index in indices for at in ends]
            text.append(jnp.zeros((taken - 2 * lines, LANES), jnp.float32))
            wide = sums_ref.shape[0] // shot_blocks
            sums_ref[i * wide : (i + 1) * wide, OWN_ROWS:, :] = jnp.broadcast_to(
                jnp.concatenate(text, axis=0)[None], (wide, taken, LANES)
            )

    def add_up(unit, both):
        row, start, stop = unit
        real, imag = both[:ROW_BLOCK], both[ROW_BLOCK:]
        logs = jnp.log((real * real + imag * imag) * inv_samples + 1e-06)
        high = logs.astype(jnp.bfloat16)
        low = (logs - high.astype(jnp.float32)).astype(jnp.bfloat16)
        sums = across(high, onehot[:, start:stop]) + across(low, onehot[:, start:stop])
        if shot_blocks:
            owners = ROW_BLOCK // OWN_ROWS
            at = (slice(row * owners, (row + 1) * owners), slice(0, OWN_ROWS), slice(None))
            sums = sums.reshape(owners, OWN_ROWS, LANES)
        else:
            at = (slice(row * ROW_BLOCK, (row + 1) * ROW_BLOCK), slice(None))
        if start == 0:
            sums_ref[at] = sums
        else:
            sums_ref[at] += sums

    def fold(start, stop):
        wide = samples // FOLDS
        parts = [traces_ref[start:stop, k * wide : (k + 1) * wide].astype(jnp.float32) for k in range(FOLDS)]
        outer, inner = parts[0] + parts[2], parts[1] + parts[3]
        for sign in sorted(set(folds)):
            total = outer + inner if sign > 0 else outer - inner
            folded_ref[sign, start:stop, :] = total.astype(jnp.bfloat16)

    units = [(place, *span) for span in spans for place in range(early)]
    units += [(place, 0, slots) for place in range(early, len(blocks))]
    before = None
    for place, start, stop in units:
        table, k = blocks[place]
        bring(blocks[place], min((stop - 1) // SLOT_BLOCK, pieces - 1))
        if folds and place == 0:
            fold(start, stop)
        if folds and table == 0:
            both = across(table_refs[0][k], folded_ref[folds[k], start:stop, :])
        else:
            both = across(table_refs[table][k], traces_ref[start:stop, :])
        if before is not None:
            add_up(*before)
        before = ((place, start, stop), both)
    add_up(*before)


def spectra_sums(traces, tables, folds, trace_shot, trace_rcv, fold_count, shot_blocks=0):
    slots, samples = traces.shape
    counts = tuple(table.shape[0] for table in tables)
    bins = sum(counts) * ROW_BLOCK
    shape = (bins // OWN_ROWS, OWN_ROWS + index_lines(slots)[1], LANES) if shot_blocks else (bins, LANES)
    in_vmem = pl.BlockSpec(memory_space=pltpu.VMEM)
    in_hbm = pl.BlockSpec(memory_space=pltpu.HBM)
    macs = sum(table.size for table in tables) * slots
    return pl.pallas_call(
        functools.partial(spectra_kernel, shot_blocks, 1.0 / samples, folds, counts),
        in_specs=[in_hbm] * (1 + len(tables)) + [in_vmem, in_vmem, pl.BlockSpec(memory_space=pltpu.SMEM)],
        out_specs=in_vmem,
        out_shape=jax.ShapeDtypeStruct(shape, jnp.float32),
        scratch_shapes=[
            pltpu.VMEM(traces.shape, traces.dtype),
            pltpu.VMEM((2, slots, samples // FOLDS), traces.dtype),
            pltpu.SemaphoreType.DMA((slots // SLOT_BLOCK,)),
        ]
        + [pltpu.VMEM(table.shape, table.dtype) for table in tables]
        + [pltpu.SemaphoreType.DMA((count,)) for count in counts],
        compiler_params=pltpu.CompilerParams(vmem_limit_bytes=WHOLE_VMEM_BYTES),
        cost_estimate=pl.CostEstimate(
            flops=2 * macs, bytes_accessed=2 * (traces.size + macs // slots), transcendentals=slots * bins
        ),
    )(traces, *tables, trace_shot, trace_rcv, fold_count)


def pairs_kernel(lines, mine_ref, other_ref, high_ref, low_ref, shot_count_ref, rcv_count_ref):
    rcv_blocks = high_ref.shape[1] // RCV_DEV
    slots = 2 * lines * LANES
    rows = lax.broadcasted_iota(jnp.int32, (SHOT_DEV, slots), 0).astype(jnp.float32).astype(jnp.bfloat16)
    one = jnp.ones((SHOT_DEV, slots), jnp.bfloat16)
    zero = jnp.zeros_like(one)
    for tile in range(mine_ref.shape[0]):
        halves = [ref[tile] for ref in (mine_ref, other_ref)]
        onehots = []
        for first in (0, lines):
            flat = [half[first + k : first + k + 1, :] for half in halves for k in range(lines)]
            onehots.append(jnp.where(jnp.concatenate(flat, axis=1).astype(jnp.bfloat16) == rows, one, zero))
        pairs = across(*onehots)
        high = pairs.astype(jnp.bfloat16)
        i, j = divmod(tile, rcv_blocks)
        place = (slice(i * SHOT_DEV, (i + 1) * SHOT_DEV), slice(j * RCV_DEV, (j + 1) * RCV_DEV))
        high_ref[place] = high
        low_ref[place] = (pairs - high.astype(jnp.float32)).astype(jnp.bfloat16)
    ones_rcv = jnp.ones((16, high_ref.shape[1]), jnp.bfloat16)
    ones_shot = jnp.ones((16, high_ref.shape[0]), jnp.bfloat16)
    shot_count_ref[...] = (across(ones_rcv, high_ref[...]) + across(ones_rcv, low_ref[...]))[:8]
    rcv_count_ref[...] = (along(ones_shot, high_ref[...]) + along(ones_shot, low_ref[...]))[:8]


def pair_counts(mine, other, lines, shot_blocks, rcv_blocks):
    shots, rcvs = shot_blocks * SHOT_DEV, rcv_blocks * RCV_DEV
    return pl.pallas_call(
        functools.partial(pairs_kernel, lines),
        out_shape=[
            jax.ShapeDtypeStruct((shots, rcvs), jnp.bfloat16),
            jax.ShapeDtypeStruct((shots, rcvs), jnp.bfloat16),
            jax.ShapeDtypeStruct((8, shots), jnp.float32),
            jax.ShapeDtypeStruct((8, rcvs), jnp.float32),
        ],
        compiler_params=pltpu.CompilerParams(vmem_limit_bytes=VMEM_BYTES),
        cost_estimate=pl.CostEstimate(
            flops=4 * shots * rcvs * lines * LANES, bytes_accessed=4 * shots * rcvs, transcendentals=0
        ),
    )(mine, other)


def solve_kernel(shot_blocks, rcv_blocks, own_rows, *refs):
    groups = len(own_rows)
    high_ref, low_ref, shot_count_ref, rcv_count_ref, out = refs[groups:]
    bins = out.shape[1] * 2 // 3

    def total(places, lanes):
        sums = [
            functools.reduce(lambda a, b: a + b, [part[k, :count, lanes] for k in places])
            for part, count in zip(refs, own_rows)
        ]
        return jnp.concatenate(sums, axis=0)

    of_shot, of_rcv = slice(0, SHOT_DEV), slice(SHOT_DEV, SHOT_DEV + RCV_DEV)
    shot_logs = jnp.concatenate(
        [total([i * rcv_blocks + j for j in range(rcv_blocks)], of_shot) for i in range(shot_blocks)], axis=1
    )
    rcv_logs = jnp.concatenate(
        [total([i * rcv_blocks + j for i in range(shot_blocks)], of_rcv) for j in range(rcv_blocks)], axis=1
    )
    shot_count = shot_count_ref[0:1, :]
    rcv_count = rcv_count_ref[0:1, :]

    def times(terms, product):
        first = terms.astype(jnp.bfloat16).astype(jnp.float32)
        rest = terms - first
        second = rest.astype(jnp.bfloat16).astype(jnp.float32)
        stack = jnp.concatenate([first, second, rest - second], axis=0).astype(jnp.bfloat16)
        out = product(stack, high_ref[...]) + product(stack, low_ref[...])
        return out[:bins] + out[bins : 2 * bins] + out[2 * bins :]

    shot_terms = shot_logs / shot_count
    rcv_terms = (rcv_logs - times(shot_terms, along)) / rcv_count
    for _ in range(SWEEPS - 1):
        shot_terms = (shot_logs - times(rcv_terms, across)) / shot_count
        rcv_terms = (rcv_logs - times(shot_terms, along)) / rcv_count
    half = bins // 2
    for i in range(shot_blocks):
        mine = rcv_terms[(i % 2) * half : (i % 2 + 1) * half]
        for j in range(rcv_blocks):
            out[i * rcv_blocks + j, :bins, :] = shot_terms[:, i * SHOT_DEV : (i + 1) * SHOT_DEV]
            out[i * rcv_blocks + j, bins:, :] = mine[:, j * RCV_DEV : (j + 1) * RCV_DEV]


def solve(parts, counts, own_rows, shot_blocks, rcv_blocks):
    return pl.pallas_call(
        functools.partial(solve_kernel, shot_blocks, rcv_blocks, own_rows),
        out_shape=jax.ShapeDtypeStruct((parts[0].shape[0], sum(own_rows) * 3 // 2, SHOT_DEV), jnp.float32),
        compiler_params=pltpu.CompilerParams(vmem_limit_bytes=VMEM_BYTES),
    )(*parts, *counts)


def turn_kernel(own_rows, even_ref, back, other, shot_out, rcv_out, shot_rows, rcv_rows):
    devices, owned = back.shape[0], back.shape[1] * 2 // 3
    mine = back[:, owned:, :]
    even = even_ref[0] == 1
    rcv_back = jnp.concatenate([jnp.where(even, mine, other[...]), jnp.where(even, other[...], mine)], axis=1)
    quarter = devices * owned // FOLDS
    for taken, rows_ref, out in ((back[:, :owned, :], shot_rows, shot_out), (rcv_back, rcv_rows, rcv_out)):
        ends = [sum(own_rows[:k]) for k in range(len(own_rows) + 1)]
        flat = [taken[:, a:b, :].reshape(devices * (b - a), out.shape[0]) for a, b in zip(ends, ends[1:])]
        flat = jnp.concatenate(flat, axis=0)
        for k, over in enumerate(QUARTERS):
            rows_ref[pl.ds(over, quarter, stride=FOLDS), :] = flat[k * quarter : (k + 1) * quarter]
        out[...] = rows_ref[...].T


def turn(even, back, other, own_rows):
    bins = back.shape[0] * back.shape[1] * 2 // 3
    return pl.pallas_call(
        functools.partial(turn_kernel, own_rows),
        in_specs=[pl.BlockSpec(memory_space=pltpu.SMEM)] + [pl.BlockSpec(memory_space=pltpu.VMEM)] * 2,
        out_shape=[
            jax.ShapeDtypeStruct((SHOT_DEV, bins), jnp.float32),
            jax.ShapeDtypeStruct((RCV_DEV, bins), jnp.float32),
        ],
        scratch_shapes=[pltpu.VMEM((bins, SHOT_DEV), jnp.float32), pltpu.VMEM((bins, RCV_DEV), jnp.float32)],
        compiler_params=pltpu.CompilerParams(vmem_limit_bytes=VMEM_BYTES),
    )(even, back, other)


def shards(traces, trace_shot, trace_rcv, fold_count):
    slot_total = traces.shape[2]
    samples_count = traces.shape[3]
    bins_count = samples_count // 2
    shot_blocks = lax.axis_size("shot")
    rcv_blocks = lax.axis_size("rcv")
    device_total = shot_blocks * rcv_blocks
    owned = bins_count // device_total
    own_rows = [OWN_ROWS] + ([owned - OWN_ROWS] if owned > OWN_ROWS else [])
    exchange = functools.partial(
        lax.all_to_all, axis_name=("shot", "rcv"), split_axis=0, concat_axis=0, tiled=True
    )
    swap = [(i, i ^ 1) for i in range(shot_blocks)]
    folded, plain = dft_tables(samples_count, bins_count)
    signs = [1] * (len(folded) // 2) + [0] * (len(folded) - len(folded) // 2)
    lines, taken = index_lines(slot_total)
    parts, at = [], 0
    for rows in own_rows:
        end = at + rows * device_total // ROW_BLOCK
        tables = [folded[at:end], plain[max(at - len(folded), 0) : max(end - len(folded), 0)]]
        sums = spectra_sums(
            traces[0, 0],
            [jnp.asarray(table) for table in tables if len(table)],
            tuple(signs[at:end]),
            trace_shot[0],
            trace_rcv[0],
            fold_count,
            0 if at else shot_blocks,
        )
        parts.append(exchange(sums if at == 0 else sums.reshape(device_total, rows, LANES)))
        at = end
    mine = parts[0][:, OWN_ROWS:, :]
    counts = pair_counts(mine, lax.ppermute(mine, "shot", swap), lines, shot_blocks, rcv_blocks)
    back = exchange(solve(parts, counts, own_rows, shot_blocks, rcv_blocks))
    other = lax.ppermute(back[:, owned:, :], "shot", swap)
    even = (1 - lax.axis_index("shot") % 2).astype(jnp.int32).reshape(1)
    return tuple(turn(even, back, other, own_rows))


def solution(mesh):
    return jax.shard_map(
        shards,
        mesh=mesh,
        in_specs=(
            P("shot", "rcv", None, None),
            P("shot", "rcv", None),
            P("shot", "rcv", None),
            P("shot", "rcv"),
        ),
        out_specs=(P("shot", None), P("rcv", None)),
        check_vma=False,
    )
```

```python
import functools

import jax
import jax.numpy as jnp
import numpy as np
from jax import lax
from jax.experimental import pallas as pl
from jax.experimental.pallas import tpu as pltpu
from jax.sharding import PartitionSpec as P

SHOT_DEV = 128
RCV_DEV = 128
SWEEPS = 3
FIRST_ROWS = 16
TILE_ROWS = 8
LANES = 128
ROW_BLOCK = 256
SLOT_BLOCK = 512
VMEM_BYTES = 40 * 1024 * 1024
WHOLE_VMEM_BYTES = 62 * 1024 * 1024


FOLDS = 4
QUARTERS = (0, 2, 1, 3)


def dft_tables(samples_count, bins_count):
    bins = np.concatenate([np.arange(over, bins_count, FOLDS) for over in QUARTERS])
    product = (bins[:, None] * np.arange(samples_count)[None, :]) % samples_count
    angle = (np.float32(2.0 * np.pi / samples_count) * product.astype(np.float32)).astype(np.float64)
    both = np.stack([np.cos(angle), np.sin(angle)]).astype(np.float32)
    both = both.reshape(2, bins_count // ROW_BLOCK, ROW_BLOCK, samples_count).transpose(1, 0, 2, 3)
    both = both.reshape(-1, 2 * ROW_BLOCK, samples_count).astype(jnp.bfloat16)
    even = bins_count // ROW_BLOCK // 2
    return both[:even, :, : samples_count // FOLDS], both[even:]


def across(a, b):
    return lax.dot_general(a, b, (((1,), (1,)), ((), ())), preferred_element_type=jnp.float32)


def along(a, b):
    return lax.dot_general(a, b, (((1,), (0,)), ((), ())), preferred_element_type=jnp.float32)


def index_lines(slots):
    lines = slots // (2 * LANES)
    return lines, -(-2 * lines // TILE_ROWS) * TILE_ROWS


def spectra_kernel(places, inv_samples, folds, counts, first, last, traces_hbm, *refs):
    shot_blocks, rcv_blocks = places
    tables = len(counts)
    table_hbms, refs = refs[:tables], refs[tables:]
    (shot_ref, rcv_ref, count_ref, core_ref), refs = refs[:4], refs[4:]
    if not first:
        earlier_ref, refs = refs[0], refs[1:]
    sums_ref, second_ref, traces_ref, folded_ref, shot_sums, rcv_sums, trace_sem = refs[:7]
    table_refs, table_sems = refs[7 : 7 + tables], refs[7 + tables :]
    slots, samples = traces_ref.shape
    pieces = slots // SLOT_BLOCK
    spans = [(k * SLOT_BLOCK, (k + 1) * SLOT_BLOCK) for k in range(pieces)]

    def trace_copy(k):
        span = pl.ds(k * SLOT_BLOCK, SLOT_BLOCK)
        return pltpu.make_async_copy(traces_hbm.at[span], traces_ref.at[span], trace_sem.at[k])

    def table_copy(table, k):
        return pltpu.make_async_copy(table_hbms[table].at[k], table_refs[table].at[k], table_sems[table].at[k])

    blocks = [(table, k) for table in range(tables) for k in range(counts[table])]
    early = min(2, len(blocks))
    order = [blocks[0], 0] + blocks[1:early] + list(range(1, pieces)) + blocks[early:]
    copies = [table_copy(*what) if isinstance(what, tuple) else trace_copy(what) for what in order]
    arrived = []

    def bring(*needed):
        while len(arrived) <= max(order.index(what) for what in needed):
            k = len(arrived)
            if k + 2 < len(copies):
                copies[k + 2].start()
            copies[k].wait()
            arrived.append(k)

    copies[0].start()
    copies[1].start()
    rows = lax.broadcasted_iota(jnp.int32, (SHOT_DEV, slots), 0)
    alive = lax.broadcasted_iota(jnp.int32, (1, slots), 1) < count_ref[0, 0]
    indices = [jnp.where(alive, ref[...], -1) for ref in (shot_ref, rcv_ref)]
    onehot = jnp.concatenate([(index == rows).astype(jnp.float32) for index in indices], axis=0).astype(jnp.bfloat16)
    owners = shot_blocks * rcv_blocks
    own = shot_sums.shape[0] // owners
    if first:
        lines, taken = index_lines(slots)
        for i in range(shot_blocks):
            ends = [(i % 2 * lines + k) * LANES for k in range(lines)]
            text = [index[:, at : at + LANES].astype(jnp.float32) for index in indices for at in ends]
            text.append(jnp.zeros((taken - 2 * lines, LANES), jnp.float32))
            sums_ref[i * rcv_blocks : (i + 1) * rcv_blocks, own : own + taken, :] = jnp.broadcast_to(
                jnp.concatenate(text, axis=0)[None], (rcv_blocks, taken, LANES)
            )

    def add_up(unit, both):
        row, start, stop = unit
        real, imag = both[:ROW_BLOCK], both[ROW_BLOCK:]
        logs = jnp.log((real * real + imag * imag) * inv_samples + 1e-06)
        high = logs.astype(jnp.bfloat16)
        low = (logs - high.astype(jnp.float32)).astype(jnp.bfloat16)
        sums = across(high, onehot[:, start:stop]) + across(low, onehot[:, start:stop])
        at = slice(row * ROW_BLOCK, (row + 1) * ROW_BLOCK)
        for ref, lanes in ((shot_sums, slice(0, SHOT_DEV)), (rcv_sums, slice(SHOT_DEV, SHOT_DEV + RCV_DEV))):
            if start == 0:
                ref[at, :] = sums[:, lanes]
            else:
                ref[at, :] += sums[:, lanes]

    def fold(start, stop):
        wide = samples // FOLDS
        parts = [traces_ref[start:stop, k * wide : (k + 1) * wide].astype(jnp.float32) for k in range(FOLDS)]
        outer, inner = parts[0] + parts[2], parts[1] + parts[3]
        for sign in sorted(set(folds)):
            total = outer + inner if sign > 0 else outer - inner
            folded_ref[sign, start:stop, :] = total.astype(jnp.bfloat16)

    units = [(place, *span) for span in spans for place in range(early)]
    units += [(place, 0, slots) for place in range(early, len(blocks))]
    before = None
    for place, start, stop in units:
        table, k = blocks[place]
        bring(blocks[place], min((stop - 1) // SLOT_BLOCK, pieces - 1))
        if folds and place == 0:
            fold(start, stop)
        if folds and table == 0:
            both = across(table_refs[0][k], folded_ref[folds[k], start:stop, :])
        else:
            both = across(table_refs[table][k], traces_ref[start:stop, :])
        if before is not None:
            add_up(*before)
        before = ((place, start, stop), both)
    add_up(*before)
    sums_ref[:, :own, :] = shot_sums[...].reshape(owners, own, SHOT_DEV)
    of_rcv = rcv_sums[...].reshape(owners, own, RCV_DEV)
    if last:
        whole = of_rcv if first else jnp.concatenate([earlier_ref[...], of_rcv], axis=1)
        half = whole.shape[1] // 2
        even = core_ref[0] == 0
        low, high = whole[:, :half, :], whole[:, half:, :]
        sums_ref[:, sums_ref.shape[1] - half :, :] = jnp.where(even, low, high)
        second_ref[...] = jnp.where(even, high, low)
    else:
        second_ref[...] = of_rcv


def spectra_sums(traces, tables, folds, trace_shot, trace_rcv, fold_count, core, places, earlier, last):
    first = earlier is None
    slots, samples = traces.shape
    owners = places[0] * places[1]
    counts = tuple(table.shape[0] for table in tables)
    bins = sum(counts) * ROW_BLOCK
    own = bins // owners
    half = (own + (0 if first else earlier.shape[1])) // 2
    rows = own + (index_lines(slots)[1] if first else 0) + (half if last else 0)
    in_vmem = pl.BlockSpec(memory_space=pltpu.VMEM)
    in_hbm = pl.BlockSpec(memory_space=pltpu.HBM)
    in_smem = pl.BlockSpec(memory_space=pltpu.SMEM)
    macs = sum(table.size for table in tables) * slots
    return pl.pallas_call(
        functools.partial(spectra_kernel, places, 1.0 / samples, folds, counts, first, last),
        in_specs=[in_hbm] * (1 + len(tables)) + [in_vmem, in_vmem, in_smem, in_smem] + [in_vmem] * (not first),
        out_specs=[in_vmem, in_vmem],
        out_shape=[
            jax.ShapeDtypeStruct((owners, rows, SHOT_DEV), jnp.float32),
            jax.ShapeDtypeStruct((owners, half if last else own, RCV_DEV), jnp.float32),
        ],
        scratch_shapes=[
            pltpu.VMEM(traces.shape, traces.dtype),
            pltpu.VMEM((2, slots, samples // FOLDS), traces.dtype),
            pltpu.VMEM((bins, SHOT_DEV), jnp.float32),
            pltpu.VMEM((bins, RCV_DEV), jnp.float32),
            pltpu.SemaphoreType.DMA((slots // SLOT_BLOCK,)),
        ]
        + [pltpu.VMEM(table.shape, table.dtype) for table in tables]
        + [pltpu.SemaphoreType.DMA((count,)) for count in counts],
        compiler_params=pltpu.CompilerParams(vmem_limit_bytes=WHOLE_VMEM_BYTES),
        cost_estimate=pl.CostEstimate(
            flops=2 * macs, bytes_accessed=2 * (traces.size + macs // slots), transcendentals=slots * bins
        ),
    )(traces, *tables, trace_shot, trace_rcv, fold_count, core, *([] if first else [earlier]))


def pairs_kernel(lines, mine_ref, other_ref, high_ref, low_ref, shot_count_ref, rcv_count_ref):
    rcv_blocks = high_ref.shape[1] // RCV_DEV
    slots = 2 * lines * LANES
    rows = lax.broadcasted_iota(jnp.int32, (SHOT_DEV, slots), 0).astype(jnp.float32).astype(jnp.bfloat16)
    one = jnp.ones((SHOT_DEV, slots), jnp.bfloat16)
    zero = jnp.zeros_like(one)
    for tile in range(mine_ref.shape[0]):
        halves = [ref[tile] for ref in (mine_ref, other_ref)]
        onehots = []
        for first in (0, lines):
            flat = [half[first + k : first + k + 1, :] for half in halves for k in range(lines)]
            onehots.append(jnp.where(jnp.concatenate(flat, axis=1).astype(jnp.bfloat16) == rows, one, zero))
        pairs = across(*onehots)
        high = pairs.astype(jnp.bfloat16)
        i, j = divmod(tile, rcv_blocks)
        place = (slice(i * SHOT_DEV, (i + 1) * SHOT_DEV), slice(j * RCV_DEV, (j + 1) * RCV_DEV))
        high_ref[place] = high
        low_ref[place] = (pairs - high.astype(jnp.float32)).astype(jnp.bfloat16)
    ones_rcv = jnp.ones((16, high_ref.shape[1]), jnp.bfloat16)
    ones_shot = jnp.ones((16, high_ref.shape[0]), jnp.bfloat16)
    shot_count_ref[...] = (across(ones_rcv, high_ref[...]) + across(ones_rcv, low_ref[...]))[:8]
    rcv_count_ref[...] = (along(ones_shot, high_ref[...]) + along(ones_shot, low_ref[...]))[:8]


def pair_counts(mine, other, lines, shot_blocks, rcv_blocks):
    shots, rcvs = shot_blocks * SHOT_DEV, rcv_blocks * RCV_DEV
    return pl.pallas_call(
        functools.partial(pairs_kernel, lines),
        out_shape=[
            jax.ShapeDtypeStruct((shots, rcvs), jnp.bfloat16),
            jax.ShapeDtypeStruct((shots, rcvs), jnp.bfloat16),
            jax.ShapeDtypeStruct((8, shots), jnp.float32),
            jax.ShapeDtypeStruct((8, rcvs), jnp.float32),
        ],
        compiler_params=pltpu.CompilerParams(vmem_limit_bytes=VMEM_BYTES),
        cost_estimate=pl.CostEstimate(
            flops=4 * shots * rcvs * lines * LANES, bytes_accessed=4 * shots * rcvs, transcendentals=0
        ),
    )(mine, other)


def solve_kernel(shot_blocks, rcv_blocks, own_rows, *refs):
    groups = len(own_rows)
    high_ref, low_ref, shot_count_ref, rcv_count_ref, out = refs[groups:]
    bins = out.shape[1] * 2 // 3

    def total(terms):
        return functools.reduce(lambda a, b: a + b, terms)

    def shot_sum(i):
        tiles = range(i * rcv_blocks, (i + 1) * rcv_blocks)
        return jnp.concatenate(
            [total([part[k, :count, :] for k in tiles]) for part, count in zip(refs, own_rows)], axis=0
        )

    def rcv_sum(j):
        at = slice(refs[groups - 1].shape[1] - bins // 2, refs[groups - 1].shape[1])
        halves = [range(parity, shot_blocks, 2) for parity in range(2)]
        return jnp.concatenate(
            [total([refs[groups - 1][i * rcv_blocks + j, at, :] for i in half]) for half in halves], axis=0
        )

    shot_logs = jnp.concatenate([shot_sum(i) for i in range(shot_blocks)], axis=1)
    rcv_logs = jnp.concatenate([rcv_sum(j) for j in range(rcv_blocks)], axis=1)
    shot_count = shot_count_ref[0:1, :]
    rcv_count = rcv_count_ref[0:1, :]

    def times(terms, product):
        first = terms.astype(jnp.bfloat16).astype(jnp.float32)
        rest = terms - first
        second = rest.astype(jnp.bfloat16).astype(jnp.float32)
        stack = jnp.concatenate([first, second, rest - second], axis=0).astype(jnp.bfloat16)
        out = product(stack, high_ref[...]) + product(stack, low_ref[...])
        return out[:bins] + out[bins : 2 * bins] + out[2 * bins :]

    shot_terms = shot_logs / shot_count
    rcv_terms = (rcv_logs - times(shot_terms, along)) / rcv_count
    for _ in range(SWEEPS - 1):
        shot_terms = (shot_logs - times(rcv_terms, across)) / shot_count
        rcv_terms = (rcv_logs - times(shot_terms, along)) / rcv_count
    half = bins // 2
    for i in range(shot_blocks):
        mine = rcv_terms[(i % 2) * half : (i % 2 + 1) * half]
        for j in range(rcv_blocks):
            out[i * rcv_blocks + j, :bins, :] = shot_terms[:, i * SHOT_DEV : (i + 1) * SHOT_DEV]
            out[i * rcv_blocks + j, bins:, :] = mine[:, j * RCV_DEV : (j + 1) * RCV_DEV]


def solve(parts, counts, own_rows, shot_blocks, rcv_blocks):
    return pl.pallas_call(
        functools.partial(solve_kernel, shot_blocks, rcv_blocks, own_rows),
        out_shape=jax.ShapeDtypeStruct((parts[0].shape[0], sum(own_rows) * 3 // 2, SHOT_DEV), jnp.float32),
        compiler_params=pltpu.CompilerParams(vmem_limit_bytes=VMEM_BYTES),
    )(*parts, *counts)


def turn_kernel(own_rows, core_ref, back, other, shot_out, rcv_out, shot_rows, rcv_rows):
    devices, owned = back.shape[0], back.shape[1] * 2 // 3
    mine = back[:, owned:, :]
    even = core_ref[0] == 0
    rcv_back = jnp.concatenate([jnp.where(even, mine, other[...]), jnp.where(even, other[...], mine)], axis=1)
    quarter = devices * owned // FOLDS
    for taken, rows_ref, out in ((back[:, :owned, :], shot_rows, shot_out), (rcv_back, rcv_rows, rcv_out)):
        ends = [sum(own_rows[:k]) for k in range(len(own_rows) + 1)]
        flat = [taken[:, a:b, :].reshape(devices * (b - a), out.shape[0]) for a, b in zip(ends, ends[1:])]
        flat = jnp.concatenate(flat, axis=0)
        for k, over in enumerate(QUARTERS):
            rows_ref[pl.ds(over, quarter, stride=FOLDS), :] = flat[k * quarter : (k + 1) * quarter]
        out[...] = rows_ref[...].T


def turn(core, back, other, own_rows):
    bins = back.shape[0] * back.shape[1] * 2 // 3
    return pl.pallas_call(
        functools.partial(turn_kernel, own_rows),
        in_specs=[pl.BlockSpec(memory_space=pltpu.SMEM)] + [pl.BlockSpec(memory_space=pltpu.VMEM)] * 2,
        out_shape=[
            jax.ShapeDtypeStruct((SHOT_DEV, bins), jnp.float32),
            jax.ShapeDtypeStruct((RCV_DEV, bins), jnp.float32),
        ],
        scratch_shapes=[pltpu.VMEM((bins, SHOT_DEV), jnp.float32), pltpu.VMEM((bins, RCV_DEV), jnp.float32)],
        compiler_params=pltpu.CompilerParams(vmem_limit_bytes=VMEM_BYTES),
    )(core, back, other)


def shards(traces, trace_shot, trace_rcv, fold_count):
    slot_total = traces.shape[2]
    samples_count = traces.shape[3]
    bins_count = samples_count // 2
    shot_blocks = lax.axis_size("shot")
    rcv_blocks = lax.axis_size("rcv")
    device_total = shot_blocks * rcv_blocks
    owned = bins_count // device_total
    own_rows = [FIRST_ROWS, owned - FIRST_ROWS] if owned > FIRST_ROWS else [owned]
    exchange = functools.partial(
        lax.all_to_all, axis_name=("shot", "rcv"), split_axis=0, concat_axis=0, tiled=True
    )
    swap = [(i, i ^ 1) for i in range(shot_blocks)]
    folded, plain = dft_tables(samples_count, bins_count)
    signs = [1] * (len(folded) // 2) + [0] * (len(folded) - len(folded) // 2)
    lines, taken = index_lines(slot_total)
    here = lax.axis_index("shot")
    core = (here % 2).astype(jnp.int32).reshape(1)
    parts, at, second = [], 0, None
    for k, rows in enumerate(own_rows):
        end = at + rows * device_total // ROW_BLOCK
        tables = [folded[at:end], plain[max(at - len(folded), 0) : max(end - len(folded), 0)]]
        last = k == len(own_rows) - 1
        sums, second = spectra_sums(
            traces[0, 0],
            [jnp.asarray(table) for table in tables if len(table)],
            tuple(signs[at:end]),
            trace_shot[0],
            trace_rcv[0],
            fold_count,
            core,
            (shot_blocks, rcv_blocks),
            second,
            last,
        )
        if last:
            sums = sums.at[:, sums.shape[1] - owned // 2 :, :].add(lax.ppermute(second, "shot", swap))
        parts.append(exchange(sums))
        at = end
    mine = parts[0][:, own_rows[0] : own_rows[0] + taken, :]
    counts = pair_counts(mine, lax.ppermute(mine, "shot", swap), lines, shot_blocks, rcv_blocks)
    back = exchange(solve(parts, counts, own_rows, shot_blocks, rcv_blocks))
    other = lax.ppermute(back[:, owned:, :], "shot", swap)
    return tuple(turn(core, back, other, own_rows))


def solution(mesh):
    return jax.shard_map(
        shards,
        mesh=mesh,
        in_specs=(
            P("shot", "rcv", None, None),
            P("shot", "rcv", None),
            P("shot", "rcv", None),
            P("shot", "rcv"),
        ),
        out_specs=(P("shot", None), P("rcv", None)),
        check_vma=False,
    )
```

```python
import functools

import jax
import jax.numpy as jnp
import numpy as np
from jax import lax
from jax.experimental import pallas as pl
from jax.experimental.pallas import tpu as pltpu
from jax.sharding import PartitionSpec as P

SHOT_DEV = 128
RCV_DEV = 128
SWEEPS = 3
FIRST_ROWS = 16
TILE_ROWS = 8
LANES = 128
ROW_BLOCK = 256
SLOT_BLOCK = 512
VMEM_BYTES = 40 * 1024 * 1024
WHOLE_VMEM_BYTES = 62 * 1024 * 1024


FOLDS = 4
QUARTERS = (0, 2, 1, 3)


FOLDS = 4
QUARTERS = (0, 2, 1, 3)
SPANS = (4, 4, 2, 1)


def dft_tables(samples_count, bins_count):
    tables = []
    for over, span in zip(QUARTERS, SPANS):
        bins = np.arange(over, bins_count, FOLDS)
        product = (bins[:, None] * np.arange(samples_count // span)[None, :]) % samples_count
        angle = (np.float32(2.0 * np.pi / samples_count) * product.astype(np.float32)).astype(np.float64)
        both = np.stack([np.cos(angle), np.sin(angle)]).astype(np.float32)
        both = both.reshape(2, len(bins) // ROW_BLOCK, ROW_BLOCK, -1).transpose(1, 0, 2, 3)
        tables.append(both.reshape(len(both), 2 * ROW_BLOCK, -1).astype(jnp.bfloat16))
    return tables


def across(a, b):
    return lax.dot_general(a, b, (((1,), (1,)), ((), ())), preferred_element_type=jnp.float32)


def along(a, b):
    return lax.dot_general(a, b, (((1,), (0,)), ((), ())), preferred_element_type=jnp.float32)


def index_lines(slots):
    lines = slots // (2 * LANES)
    return lines, -(-2 * lines // TILE_ROWS) * TILE_ROWS


def spectra_kernel(places, inv_samples, kinds, counts, first, last, traces_hbm, *refs):
    shot_blocks, rcv_blocks = places
    tables = len(counts)
    table_hbms, refs = refs[:tables], refs[tables:]
    (shot_ref, rcv_ref, count_ref, core_ref), refs = refs[:4], refs[4:]
    if not first:
        earlier_ref, refs = refs[0], refs[1:]
    sums_ref, second_ref, traces_ref, folded_ref, halved_ref, shot_sums, rcv_sums, trace_sem = refs[:8]
    table_refs, table_sems = refs[8 : 8 + tables], refs[8 + tables :]
    slots, samples = traces_ref.shape
    pieces = slots // SLOT_BLOCK
    spans = [(k * SLOT_BLOCK, (k + 1) * SLOT_BLOCK) for k in range(pieces)]

    def trace_copy(k):
        span = pl.ds(k * SLOT_BLOCK, SLOT_BLOCK)
        return pltpu.make_async_copy(traces_hbm.at[span], traces_ref.at[span], trace_sem.at[k])

    def table_copy(table, k):
        return pltpu.make_async_copy(table_hbms[table].at[k], table_refs[table].at[k], table_sems[table].at[k])

    blocks = [(table, k) for table in range(tables) for k in range(counts[table])]
    early = min(2, len(blocks))
    order = [blocks[0], 0] + blocks[1:early] + list(range(1, pieces)) + blocks[early:]
    copies = [table_copy(*what) if isinstance(what, tuple) else trace_copy(what) for what in order]
    arrived = []

    def bring(*needed):
        while len(arrived) <= max(order.index(what) for what in needed):
            k = len(arrived)
            if k + 2 < len(copies):
                copies[k + 2].start()
            copies[k].wait()
            arrived.append(k)

    copies[0].start()
    copies[1].start()
    rows = lax.broadcasted_iota(jnp.int32, (SHOT_DEV, slots), 0)
    alive = lax.broadcasted_iota(jnp.int32, (1, slots), 1) < count_ref[0, 0]
    indices = [jnp.where(alive, ref[...], -1) for ref in (shot_ref, rcv_ref)]
    onehot = jnp.concatenate([(index == rows).astype(jnp.float32) for index in indices], axis=0).astype(jnp.bfloat16)
    owners = shot_blocks * rcv_blocks
    own = shot_sums.shape[0] // owners
    if first:
        lines, taken = index_lines(slots)
        for i in range(shot_blocks):
            ends = [(i % 2 * lines + k) * LANES for k in range(lines)]
            text = [index[:, at : at + LANES].astype(jnp.float32) for index in indices for at in ends]
            text.append(jnp.zeros((taken - 2 * lines, LANES), jnp.float32))
            sums_ref[i * rcv_blocks : (i + 1) * rcv_blocks, own : own + taken, :] = jnp.broadcast_to(
                jnp.concatenate(text, axis=0)[None], (rcv_blocks, taken, LANES)
            )

    def add_up(unit, both):
        row, start, stop = unit
        real, imag = both[:ROW_BLOCK], both[ROW_BLOCK:]
        logs = jnp.log((real * real + imag * imag) * inv_samples + 1e-06)
        high = logs.astype(jnp.bfloat16)
        low = (logs - high.astype(jnp.float32)).astype(jnp.bfloat16)
        sums = across(high, onehot[:, start:stop]) + across(low, onehot[:, start:stop])
        at = slice(row * ROW_BLOCK, (row + 1) * ROW_BLOCK)
        for ref, lanes in ((shot_sums, slice(0, SHOT_DEV)), (rcv_sums, slice(SHOT_DEV, SHOT_DEV + RCV_DEV))):
            if start == 0:
                ref[at, :] = sums[:, lanes]
            else:
                ref[at, :] += sums[:, lanes]

    def fold(start, stop):
        wide = samples // FOLDS
        parts = [traces_ref[start:stop, k * wide : (k + 1) * wide].astype(jnp.float32) for k in range(FOLDS)]
        for kind in kinds:
            if kind < 2:
                outer, inner = parts[0] + parts[2], parts[1] + parts[3]
                total = outer + inner if kind == 0 else outer - inner
                folded_ref[kind, start:stop, :] = total.astype(jnp.bfloat16)
            elif kind == 2:
                halved_ref[start:stop, :wide] = (parts[0] - parts[2]).astype(jnp.bfloat16)
                halved_ref[start:stop, wide:] = (parts[1] - parts[3]).astype(jnp.bfloat16)

    def folded(kind, start, stop):
        if kind < 2:
            return folded_ref[kind, start:stop, :]
        return (halved_ref if kind == 2 else traces_ref)[start:stop, :]

    units = [(place, *span) for span in spans for place in range(early)]
    units += [(place, 0, slots) for place in range(early, len(blocks))]
    before = None
    for place, start, stop in units:
        table, k = blocks[place]
        bring(blocks[place], min((stop - 1) // SLOT_BLOCK, pieces - 1))
        if place == 0:
            fold(start, stop)
        both = across(table_refs[table][k], folded(kinds[table], start, stop))
        if before is not None:
            add_up(*before)
        before = ((place, start, stop), both)
    add_up(*before)
    sums_ref[:, :own, :] = shot_sums[...].reshape(owners, own, SHOT_DEV)
    of_rcv = rcv_sums[...].reshape(owners, own, RCV_DEV)
    if last:
        whole = of_rcv if first else jnp.concatenate([earlier_ref[...], of_rcv], axis=1)
        half = whole.shape[1] // 2
        even = core_ref[0] == 0
        low, high = whole[:, :half, :], whole[:, half:, :]
        sums_ref[:, sums_ref.shape[1] - half :, :] = jnp.where(even, low, high)
        second_ref[...] = jnp.where(even, high, low)
    else:
        second_ref[...] = of_rcv


def spectra_sums(traces, tables, kinds, trace_shot, trace_rcv, fold_count, core, places, earlier, last):
    first = earlier is None
    slots, samples = traces.shape
    owners = places[0] * places[1]
    counts = tuple(table.shape[0] for table in tables)
    bins = sum(counts) * ROW_BLOCK
    own = bins // owners
    half = (own + (0 if first else earlier.shape[1])) // 2
    rows = own + (index_lines(slots)[1] if first else 0) + (half if last else 0)
    in_vmem = pl.BlockSpec(memory_space=pltpu.VMEM)
    in_hbm = pl.BlockSpec(memory_space=pltpu.HBM)
    in_smem = pl.BlockSpec(memory_space=pltpu.SMEM)
    macs = sum(table.size for table in tables) * slots
    return pl.pallas_call(
        functools.partial(spectra_kernel, places, 1.0 / samples, kinds, counts, first, last),
        in_specs=[in_hbm] * (1 + len(tables)) + [in_vmem, in_vmem, in_smem, in_smem] + [in_vmem] * (not first),
        out_specs=[in_vmem, in_vmem],
        out_shape=[
            jax.ShapeDtypeStruct((owners, rows, SHOT_DEV), jnp.float32),
            jax.ShapeDtypeStruct((owners, half if last else own, RCV_DEV), jnp.float32),
        ],
        scratch_shapes=[
            pltpu.VMEM(traces.shape, traces.dtype),
            pltpu.VMEM((2, slots, samples // FOLDS), traces.dtype),
            pltpu.VMEM((slots, samples // 2), traces.dtype),
            pltpu.VMEM((bins, SHOT_DEV), jnp.float32),
            pltpu.VMEM((bins, RCV_DEV), jnp.float32),
            pltpu.SemaphoreType.DMA((slots // SLOT_BLOCK,)),
        ]
        + [pltpu.VMEM(table.shape, table.dtype) for table in tables]
        + [pltpu.SemaphoreType.DMA((count,)) for count in counts],
        compiler_params=pltpu.CompilerParams(vmem_limit_bytes=WHOLE_VMEM_BYTES),
        cost_estimate=pl.CostEstimate(
            flops=2 * macs, bytes_accessed=2 * (traces.size + macs // slots), transcendentals=slots * bins
        ),
    )(traces, *tables, trace_shot, trace_rcv, fold_count, core, *([] if first else [earlier]))


def pairs_kernel(lines, mine_ref, other_ref, high_ref, low_ref, shot_count_ref, rcv_count_ref):
    rcv_blocks = high_ref.shape[1] // RCV_DEV
    slots = 2 * lines * LANES
    rows = lax.broadcasted_iota(jnp.int32, (SHOT_DEV, slots), 0).astype(jnp.float32).astype(jnp.bfloat16)
    one = jnp.ones((SHOT_DEV, slots), jnp.bfloat16)
    zero = jnp.zeros_like(one)
    for tile in range(mine_ref.shape[0]):
        halves = [ref[tile] for ref in (mine_ref, other_ref)]
        onehots = []
        for first in (0, lines):
            flat = [half[first + k : first + k + 1, :] for half in halves for k in range(lines)]
            onehots.append(jnp.where(jnp.concatenate(flat, axis=1).astype(jnp.bfloat16) == rows, one, zero))
        pairs = across(*onehots)
        high = pairs.astype(jnp.bfloat16)
        i, j = divmod(tile, rcv_blocks)
        place = (slice(i * SHOT_DEV, (i + 1) * SHOT_DEV), slice(j * RCV_DEV, (j + 1) * RCV_DEV))
        high_ref[place] = high
        low_ref[place] = (pairs - high.astype(jnp.float32)).astype(jnp.bfloat16)
    ones_rcv = jnp.ones((16, high_ref.shape[1]), jnp.bfloat16)
    ones_shot = jnp.ones((16, high_ref.shape[0]), jnp.bfloat16)
    shot_count_ref[...] = (across(ones_rcv, high_ref[...]) + across(ones_rcv, low_ref[...]))[:8]
    rcv_count_ref[...] = (along(ones_shot, high_ref[...]) + along(ones_shot, low_ref[...]))[:8]


def pair_counts(mine, other, lines, shot_blocks, rcv_blocks):
    shots, rcvs = shot_blocks * SHOT_DEV, rcv_blocks * RCV_DEV
    return pl.pallas_call(
        functools.partial(pairs_kernel, lines),
        out_shape=[
            jax.ShapeDtypeStruct((shots, rcvs), jnp.bfloat16),
            jax.ShapeDtypeStruct((shots, rcvs), jnp.bfloat16),
            jax.ShapeDtypeStruct((8, shots), jnp.float32),
            jax.ShapeDtypeStruct((8, rcvs), jnp.float32),
        ],
        compiler_params=pltpu.CompilerParams(vmem_limit_bytes=VMEM_BYTES),
        cost_estimate=pl.CostEstimate(
            flops=4 * shots * rcvs * lines * LANES, bytes_accessed=4 * shots * rcvs, transcendentals=0
        ),
    )(mine, other)


def solve_kernel(shot_blocks, rcv_blocks, own_rows, *refs):
    groups = len(own_rows)
    high_ref, low_ref, shot_count_ref, rcv_count_ref, out = refs[groups:]
    bins = out.shape[1] * 2 // 3

    def total(terms):
        return functools.reduce(lambda a, b: a + b, terms)

    def shot_sum(i):
        tiles = range(i * rcv_blocks, (i + 1) * rcv_blocks)
        return jnp.concatenate(
            [total([part[k, :count, :] for k in tiles]) for part, count in zip(refs, own_rows)], axis=0
        )

    def rcv_sum(j):
        at = slice(refs[groups - 1].shape[1] - bins // 2, refs[groups - 1].shape[1])
        halves = [range(parity, shot_blocks, 2) for parity in range(2)]
        return jnp.concatenate(
            [total([refs[groups - 1][i * rcv_blocks + j, at, :] for i in half]) for half in halves], axis=0
        )

    shot_logs = jnp.concatenate([shot_sum(i) for i in range(shot_blocks)], axis=1)
    rcv_logs = jnp.concatenate([rcv_sum(j) for j in range(rcv_blocks)], axis=1)
    shot_count = shot_count_ref[0:1, :]
    rcv_count = rcv_count_ref[0:1, :]

    def times(terms, product):
        first = terms.astype(jnp.bfloat16).astype(jnp.float32)
        rest = terms - first
        second = rest.astype(jnp.bfloat16).astype(jnp.float32)
        stack = jnp.concatenate([first, second, rest - second], axis=0).astype(jnp.bfloat16)
        out = product(stack, high_ref[...]) + product(stack, low_ref[...])
        return out[:bins] + out[bins : 2 * bins] + out[2 * bins :]

    shot_terms = shot_logs / shot_count
    rcv_terms = (rcv_logs - times(shot_terms, along)) / rcv_count
    for _ in range(SWEEPS - 1):
        shot_terms = (shot_logs - times(rcv_terms, across)) / shot_count
        rcv_terms = (rcv_logs - times(shot_terms, along)) / rcv_count
    half = bins // 2
    for i in range(shot_blocks):
        mine = rcv_terms[(i % 2) * half : (i % 2 + 1) * half]
        for j in range(rcv_blocks):
            out[i * rcv_blocks + j, :bins, :] = shot_terms[:, i * SHOT_DEV : (i + 1) * SHOT_DEV]
            out[i * rcv_blocks + j, bins:, :] = mine[:, j * RCV_DEV : (j + 1) * RCV_DEV]


def solve(parts, counts, own_rows, shot_blocks, rcv_blocks):
    return pl.pallas_call(
        functools.partial(solve_kernel, shot_blocks, rcv_blocks, own_rows),
        out_shape=jax.ShapeDtypeStruct((parts[0].shape[0], sum(own_rows) * 3 // 2, SHOT_DEV), jnp.float32),
        compiler_params=pltpu.CompilerParams(vmem_limit_bytes=VMEM_BYTES),
    )(*parts, *counts)


def turn_kernel(own_rows, core_ref, back, other, shot_out, rcv_out, shot_rows, rcv_rows):
    devices, owned = back.shape[0], back.shape[1] * 2 // 3
    mine = back[:, owned:, :]
    even = core_ref[0] == 0
    rcv_back = jnp.concatenate([jnp.where(even, mine, other[...]), jnp.where(even, other[...], mine)], axis=1)
    quarter = devices * owned // FOLDS
    for taken, rows_ref, out in ((back[:, :owned, :], shot_rows, shot_out), (rcv_back, rcv_rows, rcv_out)):
        ends = [sum(own_rows[:k]) for k in range(len(own_rows) + 1)]
        flat = [taken[:, a:b, :].reshape(devices * (b - a), out.shape[0]) for a, b in zip(ends, ends[1:])]
        flat = jnp.concatenate(flat, axis=0)
        for k, over in enumerate(QUARTERS):
            rows_ref[pl.ds(over, quarter, stride=FOLDS), :] = flat[k * quarter : (k + 1) * quarter]
        out[...] = rows_ref[...].T


def turn(core, back, other, own_rows):
    bins = back.shape[0] * back.shape[1] * 2 // 3
    return pl.pallas_call(
        functools.partial(turn_kernel, own_rows),
        in_specs=[pl.BlockSpec(memory_space=pltpu.SMEM)] + [pl.BlockSpec(memory_space=pltpu.VMEM)] * 2,
        out_shape=[
            jax.ShapeDtypeStruct((SHOT_DEV, bins), jnp.float32),
            jax.ShapeDtypeStruct((RCV_DEV, bins), jnp.float32),
        ],
        scratch_shapes=[pltpu.VMEM((bins, SHOT_DEV), jnp.float32), pltpu.VMEM((bins, RCV_DEV), jnp.float32)],
        compiler_params=pltpu.CompilerParams(vmem_limit_bytes=VMEM_BYTES),
    )(core, back, other)


def shards(traces, trace_shot, trace_rcv, fold_count):
    slot_total = traces.shape[2]
    samples_count = traces.shape[3]
    bins_count = samples_count // 2
    shot_blocks = lax.axis_size("shot")
    rcv_blocks = lax.axis_size("rcv")
    device_total = shot_blocks * rcv_blocks
    owned = bins_count // device_total
    own_rows = [FIRST_ROWS, owned - FIRST_ROWS] if owned > FIRST_ROWS else [owned]
    exchange = functools.partial(
        lax.all_to_all, axis_name=("shot", "rcv"), split_axis=0, concat_axis=0, tiled=True
    )
    swap = [(i, i ^ 1) for i in range(shot_blocks)]
    tables = dft_tables(samples_count, bins_count)
    lines, taken = index_lines(slot_total)
    here = lax.axis_index("shot")
    core = (here % 2).astype(jnp.int32).reshape(1)
    parts, at, second = [], 0, None
    for k, rows in enumerate(own_rows):
        end = at + rows * device_total // ROW_BLOCK
        used = []
        for kind, table in enumerate(tables):
            start = kind * len(table)
            used.append((kind, table[max(at - start, 0) : max(end - start, 0)]))
        used = [(kind, jnp.asarray(table)) for kind, table in used if len(table)]
        last = k == len(own_rows) - 1
        sums, second = spectra_sums(
            traces[0, 0],
            [table for _, table in used],
            tuple(kind for kind, _ in used),
            trace_shot[0],
            trace_rcv[0],
            fold_count,
            core,
            (shot_blocks, rcv_blocks),
            second,
            last,
        )
        if last:
            sums = sums.at[:, sums.shape[1] - owned // 2 :, :].add(lax.ppermute(second, "shot", swap))
        parts.append(exchange(sums))
        at = end
    mine = parts[0][:, own_rows[0] : own_rows[0] + taken, :]
    counts = pair_counts(mine, lax.ppermute(mine, "shot", swap), lines, shot_blocks, rcv_blocks)
    back = exchange(solve(parts, counts, own_rows, shot_blocks, rcv_blocks))
    other = lax.ppermute(back[:, owned:, :], "shot", swap)
    return tuple(turn(core, back, other, own_rows))


def solution(mesh):
    return jax.shard_map(
        shards,
        mesh=mesh,
        in_specs=(
            P("shot", "rcv", None, None),
            P("shot", "rcv", None),
            P("shot", "rcv", None),
            P("shot", "rcv"),
        ),
        out_specs=(P("shot", None), P("rcv", None)),
        check_vma=False,
    )
```

```python
import functools

import jax
import jax.numpy as jnp
import numpy as np
from jax import lax
from jax.experimental import pallas as pl
from jax.experimental.pallas import tpu as pltpu
from jax.sharding import PartitionSpec as P

SHOT_DEV = 128
RCV_DEV = 128
SWEEPS = 3
FIRST_ROWS = 16
TILE_ROWS = 8
LANES = 128
ROW_BLOCK = 256
SLOT_BLOCK = 512
DEPTH = 3
VMEM_BYTES = 40 * 1024 * 1024
WHOLE_VMEM_BYTES = 62 * 1024 * 1024


FOLDS = 4
QUARTERS = (0, 2, 1, 3)


FOLDS = 4
QUARTERS = (0, 2, 1, 3)
SPANS = (4, 4, 2, 1)


def dft_tables(samples_count, bins_count):
    tables = []
    for over, span in zip(QUARTERS, SPANS):
        bins = np.arange(over, bins_count, FOLDS)
        product = (bins[:, None] * np.arange(samples_count // span)[None, :]) % samples_count
        angle = (np.float32(2.0 * np.pi / samples_count) * product.astype(np.float32)).astype(np.float64)
        both = np.stack([np.cos(angle), np.sin(angle)]).astype(np.float32)
        both = both.reshape(2, len(bins) // ROW_BLOCK, ROW_BLOCK, -1).transpose(1, 0, 2, 3)
        tables.append(both.reshape(len(both), 2 * ROW_BLOCK, -1).astype(jnp.bfloat16))
    return tables


def across(a, b):
    return lax.dot_general(a, b, (((1,), (1,)), ((), ())), preferred_element_type=jnp.float32)


def along(a, b):
    return lax.dot_general(a, b, (((1,), (0,)), ((), ())), preferred_element_type=jnp.float32)


def index_lines(slots):
    lines = slots // (2 * LANES)
    return lines, -(-2 * lines // TILE_ROWS) * TILE_ROWS


def spectra_kernel(places, inv_samples, kinds, counts, first, last, traces_hbm, *refs):
    shot_blocks, rcv_blocks = places
    tables = len(counts)
    table_hbms, refs = refs[:tables], refs[tables:]
    (shot_ref, rcv_ref, count_ref, core_ref), refs = refs[:4], refs[4:]
    if not first:
        earlier_ref, refs = refs[0], refs[1:]
    sums_ref, second_ref, traces_ref, folded_ref, halved_ref, shot_sums, rcv_sums, trace_sem = refs[:8]
    table_refs, table_sems = refs[8 : 8 + tables], refs[8 + tables :]
    slots, samples = traces_ref.shape
    pieces = slots // SLOT_BLOCK
    spans = [(k * SLOT_BLOCK, (k + 1) * SLOT_BLOCK) for k in range(pieces)]

    def trace_copy(k):
        span = pl.ds(k * SLOT_BLOCK, SLOT_BLOCK)
        return pltpu.make_async_copy(traces_hbm.at[span], traces_ref.at[span], trace_sem.at[k])

    def table_copy(table, k):
        return pltpu.make_async_copy(table_hbms[table].at[k], table_refs[table].at[k], table_sems[table].at[k])

    blocks = [(table, k) for table in range(tables) for k in range(counts[table])]
    early = min(2, len(blocks))
    order = [blocks[0], 0] + blocks[1:early] + list(range(1, pieces)) + blocks[early:]
    copies = [table_copy(*what) if isinstance(what, tuple) else trace_copy(what) for what in order]
    arrived = []

    def bring(*needed):
        while len(arrived) <= max(order.index(what) for what in needed):
            k = len(arrived)
            if k + DEPTH < len(copies):
                copies[k + DEPTH].start()
            copies[k].wait()
            arrived.append(k)

    for copy in copies[:DEPTH]:
        copy.start()
    rows = lax.broadcasted_iota(jnp.int32, (SHOT_DEV, slots), 0)
    alive = lax.broadcasted_iota(jnp.int32, (1, slots), 1) < count_ref[0, 0]
    indices = [jnp.where(alive, ref[...], -1) for ref in (shot_ref, rcv_ref)]
    onehot = jnp.concatenate([(index == rows).astype(jnp.float32) for index in indices], axis=0).astype(jnp.bfloat16)
    owners = shot_blocks * rcv_blocks
    own = shot_sums.shape[0] // owners
    if first:
        lines, taken = index_lines(slots)
        for i in range(shot_blocks):
            ends = [(i % 2 * lines + k) * LANES for k in range(lines)]
            text = [index[:, at : at + LANES].astype(jnp.float32) for index in indices for at in ends]
            text.append(jnp.zeros((taken - 2 * lines, LANES), jnp.float32))
            sums_ref[i * rcv_blocks : (i + 1) * rcv_blocks, own : own + taken, :] = jnp.broadcast_to(
                jnp.concatenate(text, axis=0)[None], (rcv_blocks, taken, LANES)
            )

    def add_up(unit, both):
        row, start, stop = unit
        real, imag = both[:ROW_BLOCK], both[ROW_BLOCK:]
        logs = jnp.log((real * real + imag * imag) * inv_samples + 1e-06)
        high = logs.astype(jnp.bfloat16)
        low = (logs - high.astype(jnp.float32)).astype(jnp.bfloat16)
        sums = across(high, onehot[:, start:stop]) + across(low, onehot[:, start:stop])
        at = slice(row * ROW_BLOCK, (row + 1) * ROW_BLOCK)
        for ref, lanes in ((shot_sums, slice(0, SHOT_DEV)), (rcv_sums, slice(SHOT_DEV, SHOT_DEV + RCV_DEV))):
            if start == 0:
                ref[at, :] = sums[:, lanes]
            else:
                ref[at, :] += sums[:, lanes]

    def fold(start, stop):
        wide = samples // FOLDS
        parts = [traces_ref[start:stop, k * wide : (k + 1) * wide].astype(jnp.float32) for k in range(FOLDS)]
        for kind in kinds:
            if kind < 2:
                outer, inner = parts[0] + parts[2], parts[1] + parts[3]
                total = outer + inner if kind == 0 else outer - inner
                folded_ref[kind, start:stop, :] = total.astype(jnp.bfloat16)
            elif kind == 2:
                halved_ref[start:stop, :wide] = (parts[0] - parts[2]).astype(jnp.bfloat16)
                halved_ref[start:stop, wide:] = (parts[1] - parts[3]).astype(jnp.bfloat16)

    def folded(kind, start, stop):
        if kind < 2:
            return folded_ref[kind, start:stop, :]
        return (halved_ref if kind == 2 else traces_ref)[start:stop, :]

    units = [(place, *span) for span in spans for place in range(early)]
    units += [(place, 0, slots) for place in range(early, len(blocks))]
    before = None
    for place, start, stop in units:
        table, k = blocks[place]
        bring(blocks[place], min((stop - 1) // SLOT_BLOCK, pieces - 1))
        if place == 0:
            fold(start, stop)
        both = across(table_refs[table][k], folded(kinds[table], start, stop))
        if before is not None:
            add_up(*before)
        before = ((place, start, stop), both)
    add_up(*before)
    sums_ref[:, :own, :] = shot_sums[...].reshape(owners, own, SHOT_DEV)
    of_rcv = rcv_sums[...].reshape(owners, own, RCV_DEV)
    if last:
        whole = of_rcv if first else jnp.concatenate([earlier_ref[...], of_rcv], axis=1)
        half = whole.shape[1] // 2
        even = core_ref[0] == 0
        low, high = whole[:, :half, :], whole[:, half:, :]
        sums_ref[:, sums_ref.shape[1] - half :, :] = jnp.where(even, low, high)
        second_ref[...] = jnp.where(even, high, low)
    else:
        second_ref[...] = of_rcv


def spectra_sums(traces, tables, kinds, trace_shot, trace_rcv, fold_count, core, places, earlier, last):
    first = earlier is None
    slots, samples = traces.shape
    owners = places[0] * places[1]
    counts = tuple(table.shape[0] for table in tables)
    bins = sum(counts) * ROW_BLOCK
    own = bins // owners
    half = (own + (0 if first else earlier.shape[1])) // 2
    rows = own + (index_lines(slots)[1] if first else 0) + (half if last else 0)
    in_vmem = pl.BlockSpec(memory_space=pltpu.VMEM)
    in_hbm = pl.BlockSpec(memory_space=pltpu.HBM)
    in_smem = pl.BlockSpec(memory_space=pltpu.SMEM)
    macs = sum(table.size for table in tables) * slots
    return pl.pallas_call(
        functools.partial(spectra_kernel, places, 1.0 / samples, kinds, counts, first, last),
        in_specs=[in_hbm] * (1 + len(tables)) + [in_vmem, in_vmem, in_smem, in_smem] + [in_vmem] * (not first),
        out_specs=[in_vmem, in_vmem],
        out_shape=[
            jax.ShapeDtypeStruct((owners, rows, SHOT_DEV), jnp.float32),
            jax.ShapeDtypeStruct((owners, half if last else own, RCV_DEV), jnp.float32),
        ],
        scratch_shapes=[
            pltpu.VMEM(traces.shape, traces.dtype),
            pltpu.VMEM((2, slots, samples // FOLDS), traces.dtype),
            pltpu.VMEM((slots, samples // 2), traces.dtype),
            pltpu.VMEM((bins, SHOT_DEV), jnp.float32),
            pltpu.VMEM((bins, RCV_DEV), jnp.float32),
            pltpu.SemaphoreType.DMA((slots // SLOT_BLOCK,)),
        ]
        + [pltpu.VMEM(table.shape, table.dtype) for table in tables]
        + [pltpu.SemaphoreType.DMA((count,)) for count in counts],
        compiler_params=pltpu.CompilerParams(vmem_limit_bytes=WHOLE_VMEM_BYTES),
        cost_estimate=pl.CostEstimate(
            flops=2 * macs, bytes_accessed=2 * (traces.size + macs // slots), transcendentals=slots * bins
        ),
    )(traces, *tables, trace_shot, trace_rcv, fold_count, core, *([] if first else [earlier]))


def pairs_kernel(lines, mine_ref, other_ref, high_ref, low_ref, shot_count_ref, rcv_count_ref):
    rcv_blocks = high_ref.shape[1] // RCV_DEV
    slots = 2 * lines * LANES
    rows = lax.broadcasted_iota(jnp.int32, (SHOT_DEV, slots), 0).astype(jnp.float32).astype(jnp.bfloat16)
    one = jnp.ones((SHOT_DEV, slots), jnp.bfloat16)
    zero = jnp.zeros_like(one)
    for tile in range(mine_ref.shape[0]):
        halves = [ref[tile] for ref in (mine_ref, other_ref)]
        onehots = []
        for first in (0, lines):
            flat = [half[first + k : first + k + 1, :] for half in halves for k in range(lines)]
            onehots.append(jnp.where(jnp.concatenate(flat, axis=1).astype(jnp.bfloat16) == rows, one, zero))
        pairs = across(*onehots)
        high = pairs.astype(jnp.bfloat16)
        i, j = divmod(tile, rcv_blocks)
        place = (slice(i * SHOT_DEV, (i + 1) * SHOT_DEV), slice(j * RCV_DEV, (j + 1) * RCV_DEV))
        high_ref[place] = high
        low_ref[place] = (pairs - high.astype(jnp.float32)).astype(jnp.bfloat16)
    ones_rcv = jnp.ones((16, high_ref.shape[1]), jnp.bfloat16)
    ones_shot = jnp.ones((16, high_ref.shape[0]), jnp.bfloat16)
    shot_count_ref[...] = (across(ones_rcv, high_ref[...]) + across(ones_rcv, low_ref[...]))[:8]
    rcv_count_ref[...] = (along(ones_shot, high_ref[...]) + along(ones_shot, low_ref[...]))[:8]


def pair_counts(mine, other, lines, shot_blocks, rcv_blocks):
    shots, rcvs = shot_blocks * SHOT_DEV, rcv_blocks * RCV_DEV
    return pl.pallas_call(
        functools.partial(pairs_kernel, lines),
        out_shape=[
            jax.ShapeDtypeStruct((shots, rcvs), jnp.bfloat16),
            jax.ShapeDtypeStruct((shots, rcvs), jnp.bfloat16),
            jax.ShapeDtypeStruct((8, shots), jnp.float32),
            jax.ShapeDtypeStruct((8, rcvs), jnp.float32),
        ],
        compiler_params=pltpu.CompilerParams(vmem_limit_bytes=VMEM_BYTES),
        cost_estimate=pl.CostEstimate(
            flops=4 * shots * rcvs * lines * LANES, bytes_accessed=4 * shots * rcvs, transcendentals=0
        ),
    )(mine, other)


def solve_kernel(shot_blocks, rcv_blocks, own_rows, *refs):
    groups = len(own_rows)
    high_ref, low_ref, shot_count_ref, rcv_count_ref, out = refs[groups:]
    bins = out.shape[1] * 2 // 3

    def total(terms):
        return functools.reduce(lambda a, b: a + b, terms)

    def shot_sum(i):
        tiles = range(i * rcv_blocks, (i + 1) * rcv_blocks)
        return jnp.concatenate(
            [total([part[k, :count, :] for k in tiles]) for part, count in zip(refs, own_rows)], axis=0
        )

    def rcv_sum(j):
        at = slice(refs[groups - 1].shape[1] - bins // 2, refs[groups - 1].shape[1])
        halves = [range(parity, shot_blocks, 2) for parity in range(2)]
        return jnp.concatenate(
            [total([refs[groups - 1][i * rcv_blocks + j, at, :] for i in half]) for half in halves], axis=0
        )

    shot_logs = jnp.concatenate([shot_sum(i) for i in range(shot_blocks)], axis=1)
    rcv_logs = jnp.concatenate([rcv_sum(j) for j in range(rcv_blocks)], axis=1)
    shot_count = shot_count_ref[0:1, :]
    rcv_count = rcv_count_ref[0:1, :]

    def times(terms, product):
        first = terms.astype(jnp.bfloat16).astype(jnp.float32)
        rest = terms - first
        second = rest.astype(jnp.bfloat16).astype(jnp.float32)
        stack = jnp.concatenate([first, second, rest - second], axis=0).astype(jnp.bfloat16)
        out = product(stack, high_ref[...]) + product(stack, low_ref[...])
        return out[:bins] + out[bins : 2 * bins] + out[2 * bins :]

    shot_terms = shot_logs / shot_count
    rcv_terms = (rcv_logs - times(shot_terms, along)) / rcv_count
    for _ in range(SWEEPS - 1):
        shot_terms = (shot_logs - times(rcv_terms, across)) / shot_count
        rcv_terms = (rcv_logs - times(shot_terms, along)) / rcv_count
    half = bins // 2
    for i in range(shot_blocks):
        mine = rcv_terms[(i % 2) * half : (i % 2 + 1) * half]
        for j in range(rcv_blocks):
            out[i * rcv_blocks + j, :bins, :] = shot_terms[:, i * SHOT_DEV : (i + 1) * SHOT_DEV]
            out[i * rcv_blocks + j, bins:, :] = mine[:, j * RCV_DEV : (j + 1) * RCV_DEV]


def solve(parts, counts, own_rows, shot_blocks, rcv_blocks):
    return pl.pallas_call(
        functools.partial(solve_kernel, shot_blocks, rcv_blocks, own_rows),
        out_shape=jax.ShapeDtypeStruct((parts[0].shape[0], sum(own_rows) * 3 // 2, SHOT_DEV), jnp.float32),
        compiler_params=pltpu.CompilerParams(vmem_limit_bytes=VMEM_BYTES),
    )(*parts, *counts)


def natural(own_rows, taken, rows_ref, out):
    devices, owned = taken.shape[0], taken.shape[1]
    quarter = devices * owned // FOLDS
    ends = [sum(own_rows[:k]) for k in range(len(own_rows) + 1)]
    flat = [taken[:, a:b, :].reshape(devices * (b - a), out.shape[0]) for a, b in zip(ends, ends[1:])]
    flat = jnp.concatenate(flat, axis=0)
    for k, over in enumerate(QUARTERS):
        rows_ref[pl.ds(over, quarter, stride=FOLDS), :] = flat[k * quarter : (k + 1) * quarter]
    out[...] = rows_ref[...].T


def turn_shot_kernel(own_rows, back, out, rows_ref):
    natural(own_rows, back[:, : sum(own_rows), :], rows_ref, out)


def turn_rcv_kernel(own_rows, core_ref, mine, other, out, rows_ref):
    even = core_ref[0] == 0
    low = jnp.where(even, mine[...], other[...])
    high = jnp.where(even, other[...], mine[...])
    natural(own_rows, jnp.concatenate([low, high], axis=1), rows_ref, out)


def turn(core, back, swap, own_rows):
    owned = sum(own_rows)
    bins = back.shape[0] * owned
    params = pltpu.CompilerParams(vmem_limit_bytes=VMEM_BYTES)
    in_vmem = pl.BlockSpec(memory_space=pltpu.VMEM)
    scratch = [pltpu.VMEM((bins, SHOT_DEV), jnp.float32)]
    mine = back[:, owned:, :]
    other = lax.ppermute(mine, "shot", swap)
    shot_out = pl.pallas_call(
        functools.partial(turn_shot_kernel, own_rows),
        in_specs=[in_vmem],
        out_shape=jax.ShapeDtypeStruct((SHOT_DEV, bins), jnp.float32),
        scratch_shapes=scratch,
        compiler_params=params,
        cost_estimate=pl.CostEstimate(flops=0, bytes_accessed=2 * back.size * 4, transcendentals=0),
    )(back)
    rcv_out = pl.pallas_call(
        functools.partial(turn_rcv_kernel, own_rows),
        in_specs=[pl.BlockSpec(memory_space=pltpu.SMEM), in_vmem, in_vmem],
        out_shape=jax.ShapeDtypeStruct((RCV_DEV, bins), jnp.float32),
        scratch_shapes=scratch,
        compiler_params=params,
    )(core, mine, other)
    return shot_out, rcv_out


def shards(traces, trace_shot, trace_rcv, fold_count):
    slot_total = traces.shape[2]
    samples_count = traces.shape[3]
    bins_count = samples_count // 2
    shot_blocks = lax.axis_size("shot")
    rcv_blocks = lax.axis_size("rcv")
    device_total = shot_blocks * rcv_blocks
    owned = bins_count // device_total
    own_rows = [FIRST_ROWS, owned - FIRST_ROWS] if owned > FIRST_ROWS else [owned]
    exchange = functools.partial(
        lax.all_to_all, axis_name=("shot", "rcv"), split_axis=0, concat_axis=0, tiled=True
    )
    swap = [(i, i ^ 1) for i in range(shot_blocks)]
    tables = dft_tables(samples_count, bins_count)
    lines, taken = index_lines(slot_total)
    here = lax.axis_index("shot")
    core = (here % 2).astype(jnp.int32).reshape(1)
    parts, at, second = [], 0, None
    for k, rows in enumerate(own_rows):
        end = at + rows * device_total // ROW_BLOCK
        used = []
        for kind, table in enumerate(tables):
            start = kind * len(table)
            used.append((kind, table[max(at - start, 0) : max(end - start, 0)]))
        used = [(kind, jnp.asarray(table)) for kind, table in used if len(table)]
        last = k == len(own_rows) - 1
        sums, second = spectra_sums(
            traces[0, 0],
            [table for _, table in used],
            tuple(kind for kind, _ in used),
            trace_shot[0],
            trace_rcv[0],
            fold_count,
            core,
            (shot_blocks, rcv_blocks),
            second,
            last,
        )
        if last:
            sums = sums.at[:, sums.shape[1] - owned // 2 :, :].add(lax.ppermute(second, "shot", swap))
        parts.append(exchange(sums))
        at = end
    mine = parts[0][:, own_rows[0] : own_rows[0] + taken, :]
    counts = pair_counts(mine, lax.ppermute(mine, "shot", swap), lines, shot_blocks, rcv_blocks)
    back = exchange(solve(parts, counts, own_rows, shot_blocks, rcv_blocks))
    return turn(core, back, swap, own_rows)


def solution(mesh):
    return jax.shard_map(
        shards,
        mesh=mesh,
        in_specs=(
            P("shot", "rcv", None, None),
            P("shot", "rcv", None),
            P("shot", "rcv", None),
            P("shot", "rcv"),
        ),
        out_specs=(P("shot", None), P("rcv", None)),
        check_vma=False,
    )
```
